256 devices in a mesh: dp: 16 (over y, x), seq: 2 (over core), tensor: 8 (over z).
Axes of the slice: x: 4, y: 4, z: 8, core: 2. Of those that a mesh axis runs over, the one named last changes fastest.
Arguments:
- query_in: bfloat16 [16, 1024, 4096], P('dp', 'seq', 'tensor'), may hold values from -96 to 96
- key_in: bfloat16 [16, 1024, 4096], P('dp', 'seq', 'tensor'), may hold values from -4 to 4
- value_in: bfloat16 [16, 1024, 4096], P('dp', 'seq', 'tensor'), may hold values from -12 to 12
- attn_grad: bfloat16 [16, 1024, 4096], P('dp', 'seq', 'tensor'), may hold values from -6 to 6
- out_grad: bfloat16 [16, 1024, 4096], P('dp', 'seq', 'tensor'), may hold values from -1600 to 1600
- carried_error: float32 [16, 16, 256, 4096], P('dp', 'seq', None, 'tensor'), may hold values from -12 to 12
- lengths: int32 [16, 4], P('dp'), may hold values from 1 to 512, 1024 in all within a row
Outputs:
- d_queries: bfloat16 [16, 1024, 4096], P('dp', 'seq', 'tensor')
- d_keys: bfloat16 [16, 1024, 4096], P('dp', 'seq', 'tensor')
- d_values: bfloat16 [16, 1024, 4096], P('dp', 'seq', 'tensor')
- level_sums: float32 [16, 256, 4096], P('seq', 'dp', 'tensor')
- block_scale: float32 [16, 4096], P('seq', 'tensor')
The draws below stay inside these ranges and needn't reach their ends.
Inputs may be any that keep to these rules, and one draw needn't show every extreme that they name: Each row holds 4 image lengths that sum to 1024; one of them is exactly 512.
All inputs are finite; a program needn't handle non-finite values.
Results may differ from the reference program's by a relative error of at most 0.03.
Values may be sent and summed in bfloat16 or wider, within the bound.
No kernel may reach another device: no remote copies, remote signals or barrier semaphores. Data moves between devices by JAX's collectives and lax.ppermute only.
A program may use at most 64 MiB of HBM per device.

```python
import math
import jax
import jax.numpy as jnp
import numpy as np
from jax import lax

HEADS = 32
HEAD_DIM = 128
OUT_WIDTH = 4096
QBLOCK = 256
TOK_DEV = 512
BATCH = 16
LENGTH = 1024
MOST = 512
IMAGES = 4
BLOCKS = 16
N_SEQ = 2


def base_keys(key):
    return jnp.clip(jax.random.normal(key, (BATCH, LENGTH, HEADS, HEAD_DIM), jnp.float32), -4.0, 4.0)


def draw_query_in(key, part):
    key = jax.random.fold_in(key, 5)
    own_part = jnp.clip(jax.random.normal(key, (BATCH, LENGTH, HEADS, HEAD_DIM), jnp.float32), -4.0, 4.0)
    return own_part.reshape(BATCH, LENGTH, HEADS * HEAD_DIM).astype(jnp.bfloat16)


def draw_key_in(key, part):
    shared = base_keys(key)
    return shared.reshape(BATCH, LENGTH, HEADS * HEAD_DIM).astype(jnp.bfloat16)


def draw_value_in(key, part):
    key = jax.random.fold_in(key, 3)
    key_core, key_scale = jax.random.split(key)
    core_part = jnp.clip(jax.random.normal(key_core, (BATCH, LENGTH, HEADS * HEAD_DIM), jnp.float32), -4.0, 4.0)
    col_scale = jnp.exp(jax.random.uniform(key_scale, (HEADS * HEAD_DIM,), jnp.float32, math.log(0.3), math.log(3.0)))
    return (core_part * col_scale[None, None, :]).astype(jnp.bfloat16)


def draw_out_grad(key, part):
    key = jax.random.fold_in(key, 4)
    key_core = jax.random.fold_in(key, 0)
    key_scale = jax.random.fold_in(key, 1)
    key_block = jax.random.fold_in(key, 3)
    row_place = jnp.arange(BATCH, dtype=jnp.float32)[:, None, None] / max(BATCH - 1, 1)
    block_factor = jnp.exp(jax.random.uniform(key_block, (BATCH, BLOCKS), jnp.float32, math.log(0.2), math.log(5.0)))
    block_factor = jnp.repeat(block_factor, QBLOCK, axis=1)[:, None, :]
    core_part = jnp.clip(jax.random.normal(key_core, (BATCH, LENGTH, OUT_WIDTH), jnp.float32), -4.0, 4.0)
    col_scale = jnp.exp(jax.random.uniform(key_scale, (OUT_WIDTH,), jnp.float32, math.log(0.3), math.log(3.0)))
    row_rise = jnp.power(3.0, row_place)
    return (core_part * col_scale[None, None, :] * row_rise * block_factor).astype(jnp.bfloat16)


def steps_of(rng, dims, cuts, smallest, largest):
    gain = 1.0
    for dim, blocks in cuts:
        steps = jax.random.uniform(jax.random.fold_in(jax.random.fold_in(rng, 6), dim), (blocks,), jnp.float32, smallest / len(cuts), largest / len(cuts))
        gain = gain * jnp.repeat(jnp.exp(steps), dims[dim] // blocks).reshape((-1,) + (1,) * (len(dims) - 1 - dim))
    return gain


def length_profile(count, total, most, slope):
    loads = [(1 << 20) // math.isqrt(grade ** slope) + 1 for grade in range(2, count + 1)]
    rest, counts = total - most - (count - 1), [1] * (count - 1)
    while rest > 0:
        free = [i for i in range(count - 1) if counts[i] < most]
        whole, left = sum([loads[i] for i in free]), rest
        for i in free:
            extra = min(most - counts[i], max(1, left * loads[i] // whole), rest)
            counts[i] = counts[i] + extra
            rest = rest - extra
    return np.array([most] + counts)


def uneven(key, amount, total, bound, slope):
    if amount == 2:
        one = jax.random.randint(key, (), max(1, total - bound), min(bound, total - 1) + 1)
        return jnp.stack([one, total - one])
    tallies = jnp.asarray(length_profile(amount, total, bound, slope), jnp.int32)
    twos = (amount - 1) // 2
    source_of, receiver = tallies[1:1 + 2 * twos:2], tallies[2:2 + 2 * twos:2]
    slack = jnp.minimum(source_of - 1, bound - receiver)
    passed = jax.random.randint(jax.random.fold_in(key, 1), (twos,), 0, 1 << 20) % (slack + 1)
    tallies = tallies.at[1:1 + 2 * twos:2].set(source_of - passed).at[2:2 + 2 * twos:2].set(receiver + passed)
    return tallies[jax.random.permutation(jax.random.fold_in(key, 2), amount)]


def bell_draw(rng, extent, width, limit, cuts=(), held_as=jnp.bfloat16):
    values = jax.random.normal(rng, extent, jnp.float32) * width
    if len(cuts) > 0:
        values = steps_of(rng, extent, cuts, -0.22, 0.18) * values
    return jnp.clip(values, min=-limit, max=limit).astype(held_as)


def setup_inputs(seed: int = 0) -> dict:
    splits = jax.random.split(jax.random.key(seed), 8)
    return {
        "query_in": draw_query_in(jax.random.fold_in(splits[7], 71), 0),
        "key_in": draw_key_in(jax.random.fold_in(splits[7], 71), 0),
        "value_in": draw_value_in(jax.random.fold_in(splits[7], 71), 0),
        "attn_grad": bell_draw(splits[3], (BATCH, LENGTH, HEADS * HEAD_DIM), 1.0, 6.0, ((0, 16), (1, 2), (2, 8))),
        "out_grad": draw_out_grad(jax.random.fold_in(splits[7], 71), 0),
        "carried_error": bell_draw(splits[5], (BATCH, BLOCKS, QBLOCK, HEADS * HEAD_DIM), 3.0, 12.0, ((0, 16), (1, 2), (3, 8)), jnp.float32),
        "lengths": jax.vmap(lambda own: uneven(own, IMAGES, LENGTH, MOST, 2))(jax.random.split(splits[6], BATCH)).reshape((BATCH, IMAGES)).astype(jnp.int32),
    }


NEG_FILL = -1e+30

def rounded(values):
    return lax.optimization_barrier(values.astype(jnp.bfloat16)).astype(jnp.float32)

def image_index(length_row, row_count):
    image_ends = jnp.cumsum(length_row).astype(jnp.int32)
    positions = jnp.arange(row_count, dtype=jnp.int32)
    return lax.optimization_barrier(jnp.sum((positions[:, None] >= image_ends[None, :]).astype(jnp.int32), axis=1, dtype=jnp.int32))

def head_grads(query_rows, key_rows, value_rows, grad_rows, image_ids):
    inverse = 1.0 / math.sqrt(HEAD_DIM)
    query_f32 = query_rows.astype(jnp.float32)
    key_f32 = key_rows.astype(jnp.float32)
    value_f32 = value_rows.astype(jnp.float32)
    grad_f32 = grad_rows.astype(jnp.float32)
    scores = jnp.dot(query_f32, key_f32.T, preferred_element_type=jnp.float32) * inverse
    inside = image_ids[:, None] == image_ids[None, :]
    peak_row = lax.optimization_barrier(jnp.max(jnp.where(inside, scores, NEG_FILL), axis=1))
    total_row = lax.optimization_barrier(jnp.sum(jnp.where(inside, jnp.exp(scores - peak_row[:, None]), 0.0), axis=1))
    log_total = peak_row + jnp.log(total_row)
    weights = jnp.where(inside, jnp.exp(scores - log_total[:, None]), 0.0)
    prob_bf = weights.astype(jnp.bfloat16)
    prob_f32 = prob_bf.astype(jnp.float32)
    attended = jnp.dot(prob_f32, value_f32, preferred_element_type=jnp.float32).astype(jnp.bfloat16)
    row_delta = lax.optimization_barrier(jnp.sum(grad_f32 * attended.astype(jnp.float32), axis=1))
    grad_probs = jnp.dot(grad_f32, value_f32.T, preferred_element_type=jnp.float32)
    grad_scores = (weights * (grad_probs - row_delta[:, None]) * inverse).astype(jnp.bfloat16)
    score_f32 = grad_scores.astype(jnp.float32)
    query_grad = jnp.dot(score_f32, key_f32, preferred_element_type=jnp.float32).astype(jnp.bfloat16)
    score_blocks = score_f32.reshape(N_SEQ, TOK_DEV, LENGTH)
    prob_blocks = prob_f32.reshape(N_SEQ, TOK_DEV, LENGTH)
    query_blocks = query_f32.reshape(N_SEQ, TOK_DEV, HEAD_DIM)
    grad_blocks = grad_f32.reshape(N_SEQ, TOK_DEV, HEAD_DIM)
    key_grad = lax.optimization_barrier(jnp.sum(rounded(jnp.einsum('sqk,sqd->skd', score_blocks, query_blocks)), axis=0)).astype(jnp.bfloat16)
    value_grad = lax.optimization_barrier(jnp.sum(rounded(jnp.einsum('sqk,sqd->skd', prob_blocks, grad_blocks)), axis=0)).astype(jnp.bfloat16)
    return (query_grad, key_grad, value_grad, attended)

def one_row(operands):
    query_row, key_row, value_row, grad_row, length_row = operands
    image_ids = image_index(length_row, LENGTH)

    def head_major(flat):
        return jnp.moveaxis(flat.reshape(LENGTH, HEADS, HEAD_DIM), 1, 0)

    def token_major(cube):
        return jnp.moveaxis(cube, 0, 1).reshape(LENGTH, HEADS * HEAD_DIM)

    def per_head(items):
        return head_grads(items[0], items[1], items[2], items[3], image_ids)
    results = lax.map(per_head, (head_major(query_row), head_major(key_row), head_major(value_row), head_major(grad_row)))
    return tuple((token_major(item) for item in results))

def grad_row(operands):
    attended, out_row = operands
    attend_blocks = attended.reshape(N_SEQ, TOK_DEV, HEADS * HEAD_DIM)
    out_blocks = out_row.reshape(N_SEQ, TOK_DEV, OUT_WIDTH)

    def add_block(running, pair_items):
        attend_part, out_part = pair_items
        term_part = jnp.dot(out_part.astype(jnp.float32).T, attend_part.astype(jnp.float32), preferred_element_type=jnp.float32)
        return (running + rounded(term_part), None)
    summed, _ = lax.scan(add_block, jnp.zeros((OUT_WIDTH, HEADS * HEAD_DIM), jnp.float32), (attend_blocks, out_blocks))
    return summed

def reference(query_in, key_in, value_in, attn_grad, out_grad, carried_error, lengths):
    query_grad, key_grad, value_grad, attended = lax.map(one_row, (query_in, key_in, value_in, attn_grad, lengths))
    weight_grad = lax.map(grad_row, (attended, out_grad)).reshape(BATCH, BLOCKS, QBLOCK, HEADS * HEAD_DIM)
    corrected = weight_grad + carried_error
    block_peak = lax.optimization_barrier(jnp.max(jnp.abs(corrected), axis=(0, 2)))
    block_scale = (block_peak + 1e-06) / 7.0
    levels = rounded(corrected / block_scale[None, :, None, :])
    level_sums = lax.optimization_barrier(jnp.sum(levels, axis=0))
    return (query_grad, key_grad, value_grad, level_sums, block_scale)
```

```python
import functools
import math

import jax
import jax.numpy as jnp
from jax import lax
from jax.experimental import pallas as pl
from jax.experimental.pallas import tpu as pltpu
from jax.sharding import PartitionSpec as P

HEAD_DIM = 128
NEG_FILL = -1e30
F32 = jnp.float32
BF16 = jnp.bfloat16
VMEM_LIMIT = 48 * 2**20


def dot_on(a, b, a_dim, b_dim):
    return lax.dot_general(a, b, (((a_dim,), (b_dim,)), ((), ())), preferred_element_type=F32)


def attention_kernel(
    lengths_ref, place_ref, q_ref, ko_ref, kp_ref, vo_ref, vp_ref, g_ref,
    att_ref, dq_ref, dko_ref, dkp_ref, dvo_ref, dvp_ref,
    ids_ref, dk_acc, dv_acc, *, tile,
):
    rows = q_ref.shape[0]
    inverse = 1.0 / math.sqrt(HEAD_DIM)
    to_exp2 = inverse * math.log2(math.e)
    own = place_ref[0] * rows
    other = rows - own

    def ids(positions):
        found = jnp.zeros(positions.shape, jnp.int32)
        end = jnp.int32(0)
        for image in range(4):
            end = end + lengths_ref[image]
            found = found + (positions >= end).astype(jnp.int32)
        return found

    @pl.when(pl.program_id(0) == 0)
    def _():
        positions = lax.broadcasted_iota(jnp.int32, (rows, 128), 0)
        ids_ref[:rows, :] = ids(positions + own)
        ids_ref[rows:, :] = ids(positions + other)

    k = jnp.concatenate([ko_ref[...], kp_ref[...]], 0)
    v = jnp.concatenate([vo_ref[...], vp_ref[...]], 0)
    k_t, v_t = k.T, v.T
    for i in range(rows // tile):
        part = slice(i * tile, (i + 1) * tile)
        q, g = q_ref[part, :], g_ref[part, :]
        query_ids = ids(lax.broadcasted_iota(jnp.int32, (8, tile), 1) + (own + i * tile))[:1]
        key_ids = jnp.concatenate([ids_ref[...]] * (tile // 128), 1)
        scores = jnp.where(key_ids == query_ids, dot_on(k, q, 1, 1) * to_exp2, NEG_FILL)
        peak = jnp.max(scores, axis=0, keepdims=True)
        raised = jnp.exp2(scores - peak)
        weights = raised * (1.0 / jnp.sum(raised, axis=0, keepdims=True))
        prob = weights.astype(BF16)
        att_t = dot_on(v_t, prob, 1, 0).astype(BF16).astype(F32)
        att_ref[part, :] = att_t.T.astype(BF16)
        delta = jnp.sum(g.astype(F32).T * att_t, axis=0, keepdims=True)
        grad_probs = dot_on(v, g, 1, 1)
        grad_scores = (weights * ((grad_probs - delta) * inverse)).astype(BF16)
        dq_ref[part, :] = dot_on(k_t, grad_scores, 1, 0).T.astype(BF16)
        dk = dot_on(grad_scores, q, 1, 0)
        dv = dot_on(prob, g, 1, 0)
        if i == 0:
            dk_acc[...] = dk
            dv_acc[...] = dv
        else:
            dk_acc[...] += dk
            dv_acc[...] += dv
    dko_ref[...] = dk_acc[:rows].astype(BF16)
    dkp_ref[...] = dk_acc[rows:].astype(BF16)
    dvo_ref[...] = dv_acc[:rows].astype(BF16)
    dvp_ref[...] = dv_acc[rows:].astype(BF16)


def attention(lengths, place, q, ko, kp, vo, vp, g):
    rows, width = q.shape
    heads = width // HEAD_DIM
    spec = pl.BlockSpec((rows, HEAD_DIM), lambda i, *_: (0, i))
    return pl.pallas_call(
        functools.partial(attention_kernel, tile=256),
        grid_spec=pltpu.PrefetchScalarGridSpec(
            num_scalar_prefetch=2,
            grid=(heads,),
            in_specs=[spec] * 6,
            out_specs=[spec] * 6,
            scratch_shapes=[
                pltpu.VMEM((2 * rows, 128), jnp.int32),
                pltpu.VMEM((2 * rows, HEAD_DIM), F32),
                pltpu.VMEM((2 * rows, HEAD_DIM), F32),
            ],
        ),
        out_shape=[jax.ShapeDtypeStruct((rows, width), BF16)] * 6,
        compiler_params=pltpu.CompilerParams(vmem_limit_bytes=VMEM_LIMIT),
        cost_estimate=pl.CostEstimate(
            flops=24 * rows * rows * width,
            bytes_accessed=24 * rows * width,
            transcendentals=2 * rows * rows * heads,
        ),
        name="attention",
    )(lengths, place, q, ko, kp, vo, vp, g)


def weight_kernel(place_ref, own_ref, recv_ref, att_ref, att_peer_ref, carried_ref, *refs, dp_count):
    *peak_refs, out_ref, peak_ref = refs
    step = pl.program_id(0)
    corrected = (
        dot_on(own_ref[...], att_ref[...], 0, 0)
        + dot_on(recv_ref[...], att_peer_ref[...], 0, 0)
        + carried_ref[0]
    )
    share = corrected.shape[0] // dp_count
    peak_ref[pl.ds(step, 1), :] = jnp.max(jnp.abs(corrected), axis=0, keepdims=True)
    rounded = corrected.astype(BF16)
    place = pl.ds(pl.multiple_of(step * share, share), share)
    for dest in range(dp_count):
        out_ref[dest, place, :] = rounded[dest * share : (dest + 1) * share]
    if peak_refs:

        @pl.when(step == 1)
        def _():
            peaks = jnp.concatenate([peak_ref[...]] + [ref[...] for ref in peak_refs], 0)
            high = peaks.astype(BF16).astype(F32)
            both = jnp.concatenate([high, peaks - high], 0).astype(BF16)
            for dest in range(dp_count):
                out_ref[dest, 2 * share :, :] = both


def weight_block(place, own, recv, att, att_peer, carried, peaks, dp_count):
    rows, width = att.shape
    block = carried.shape[1]
    share = block // dp_count
    out_rows = 2 * share + (16 if peaks else 0)
    whole = lambda i, *_: (0, 0)
    half = lambda i, *_: (0, i)
    return pl.pallas_call(
        functools.partial(weight_kernel, dp_count=dp_count),
        grid_spec=pltpu.PrefetchScalarGridSpec(
            num_scalar_prefetch=1,
            grid=(2,),
            in_specs=[
                pl.BlockSpec((rows, block), half),
                pl.BlockSpec((rows, block), half),
                pl.BlockSpec((rows, width), whole),
                pl.BlockSpec((rows, width), whole),
                pl.BlockSpec((1, block, width), lambda i, ref: (2 * ref[0] + i, 0, 0)),
            ]
            + [pl.BlockSpec((2, width), whole) for _ in peaks],
            out_specs=[
                pl.BlockSpec((dp_count, out_rows, width), lambda i, *_: (0, 0, 0)),
                pl.BlockSpec((2, width), whole),
            ],
        ),
        out_shape=[
            jax.ShapeDtypeStruct((dp_count, out_rows, width), BF16),
            jax.ShapeDtypeStruct((2, width), F32),
        ],
        compiler_params=pltpu.CompilerParams(vmem_limit_bytes=VMEM_LIMIT),
        cost_estimate=pl.CostEstimate(
            flops=8 * rows * block * width, bytes_accessed=16 * rows * width, transcendentals=0
        ),
        name="weight_block",
    )(place, own, recv, att, att_peer, carried, *peaks)


def finish_kernel(place_ref, last_ref, *refs):
    *sum_refs, levels_ref, scale_ref = refs
    share = levels_ref.shape[1]
    pairs = len(sum_refs) + 1
    head = 2 * share
    peaks = jnp.max(
        last_ref[:, head : head + 8, :].astype(F32) + last_ref[:, head + 8 : head + 16, :].astype(F32),
        axis=0,
    )
    scale = (peaks + 1e-6) / 7.0
    for pair in range(pairs):
        if pair == 0:
            total = jnp.sum(last_ref[:, :head, :].astype(F32), axis=0)
        else:
            total = sum_refs[pair - 1][...]
        for half in range(2):
            block = 2 * place_ref[pair] + half
            row = scale[2 * pair + half : 2 * pair + half + 1]
            scale_ref[pl.ds(block, 1), :] = row
            levels_ref[block] = total[half * share : (half + 1) * share] / row


def finish(places, last, sums):
    width = last.shape[2]
    share = sums[0].shape[0] // 2
    blocks = 2 * (len(sums) + 1)
    return pl.pallas_call(
        finish_kernel,
        in_specs=[pl.BlockSpec(memory_space=pltpu.SMEM)]
        + [pl.BlockSpec(memory_space=pltpu.VMEM)] * (1 + len(sums)),
        out_specs=[pl.BlockSpec(memory_space=pltpu.VMEM)] * 2,
        out_shape=[
            jax.ShapeDtypeStruct((blocks, share, width), F32),
            jax.ShapeDtypeStruct((blocks, width), F32),
        ],
        compiler_params=pltpu.CompilerParams(vmem_limit_bytes=VMEM_LIMIT),
        name="finish",
    )(places, last, *sums)


def body(query_in, key_in, value_in, attn_grad, out_grad, carried_error, lengths):
    dp_count = lax.axis_size("dp")
    z_count = lax.axis_size("tensor")
    seq = lax.axis_index("seq")
    z = lax.axis_index("tensor")
    up = [(i, (i + 1) % z_count) for i in range(z_count)]
    down = [(i, (i - 1) % z_count) for i in range(z_count)]
    swap = [(0, 1), (1, 0)]

    def peer(array):
        return lax.ppermute(array, "seq", swap)

    own = out_grad[0]
    half = own.shape[0] // 2
    from_down, from_up = [own], [own]
    for _ in range(3):
        from_down.append(lax.ppermute(from_down[-1], "tensor", up))
        from_up.append(lax.ppermute(from_up[-1], "tensor", down))
    farthest = jnp.concatenate(
        [
            lax.ppermute(from_down[3][:half], "tensor", up),
            lax.ppermute(from_up[3][half:], "tensor", down),
        ],
        0,
    )
    key_peer, value_peer = peer(key_in[0]), peer(value_in[0])
    seq_place = jnp.reshape(seq, (1,)).astype(jnp.int32)
    att, dq, dk_own, dk_peer, dv_own, dv_peer = attention(
        lengths[0], seq_place, query_in[0], key_in[0], key_peer, value_in[0], value_peer, attn_grad[0]
    )
    att_peer = peer(att)
    d_keys = (dk_own.astype(F32) + peer(dk_peer).astype(F32)).astype(BF16)
    d_values = (dv_own.astype(F32) + peer(dv_peer).astype(F32)).astype(BF16)

    offsets = jnp.mod(z - jnp.arange(4, dtype=jnp.int32), z_count)
    places = jnp.mod(offsets, 4)
    pairs = {
        2: (from_down[2], from_up[2]),
        1: (from_down[1], from_up[3]),
        3: (from_down[3], from_up[1]),
        0: (own, farthest),
    }
    sums, peaks = {}, {}
    for pair, (near, far) in pairs.items():
        keep_near = (offsets[pair] // 4) == seq
        mine = jnp.where(keep_near, near, far)
        recv = peer(jnp.where(keep_near, far, near))
        known = [peaks[i] for i in (1, 2, 3)] if pair == 0 else []
        terms, peaks[pair] = weight_block(
            places[pair : pair + 1], mine, recv, att, att_peer, carried_error[0], known, dp_count
        )
        shared = lax.all_to_all(terms, "dp", 0, 0, tiled=True)
        sums[pair] = shared if pair == 0 else jnp.sum(shared.astype(F32), axis=0)
    level_sums, block_scale = finish(places, sums[0], [sums[i] for i in (1, 2, 3)])
    return dq[None], d_keys[None], d_values[None], level_sums, block_scale


def solution(mesh):
    tokens = P("dp", "seq", "tensor")
    in_specs = (tokens,) * 5 + (P("dp", "seq", None, "tensor"), P("dp", None))
    out_specs = (tokens,) * 3 + (P("seq", "dp", "tensor"), P("seq", "tensor"))
    return jax.shard_map(body, mesh=mesh, in_specs=in_specs, out_specs=out_specs, check_vma=False)
```

```python
import functools
import math

import jax
import jax.numpy as jnp
from jax import lax
from jax.experimental import pallas as pl
from jax.experimental.pallas import tpu as pltpu
from jax.sharding import PartitionSpec as P

HEAD_DIM = 128
NEG_FILL = -1e30
F32 = jnp.float32
BF16 = jnp.bfloat16
MIB = 2**20
TOKEN = jax.ShapeDtypeStruct((8, 128), F32)
TOKEN_SPEC = pl.BlockSpec((8, 128), lambda i, *_: (0, 0))


def dot_on(a, b, a_dim, b_dim):
    return lax.dot_general(a, b, (((a_dim,), (b_dim,)), ((), ())), preferred_element_type=F32)


def attention_kernel(
    place_ref, kp_ref, vp_ref, q_hbm, ko_hbm, vo_hbm, g_hbm, *refs, tile, first, count
):
    att_ref, dq_ref, dko_ref, dkp_ref, dvo_ref, dvp_ref, token_ref = refs[-12:-5]
    ids_ref, dk_acc, dv_acc, held_ref, sems = refs[-5:]
    token_ref[...] = jnp.zeros_like(token_ref)
    rows = kp_ref.shape[0]
    head = pl.program_id(0)

    def fetch(step, source, index):
        column = pl.ds((first + step) * HEAD_DIM, HEAD_DIM)
        return pltpu.make_async_copy(
            source.at[:, column], held_ref.at[step, index], sems.at[step, index]
        )

    sources = (ko_hbm, q_hbm, vo_hbm, g_hbm)

    @pl.when(head == 0)
    def _():
        for step in range(count):
            for index, source in enumerate(sources):
                fetch(step, source, index).start()
    inverse = 1.0 / math.sqrt(HEAD_DIM)
    to_exp2 = inverse * math.log2(math.e)
    own = place_ref[0] * rows
    other = rows - own

    def ids(positions):
        found = jnp.zeros(positions.shape, jnp.int32)
        end = jnp.int32(0)
        for image in range(4):
            end = end + place_ref[2 + image]
            found = found + (positions >= end).astype(jnp.int32)
        return found

    @pl.when(head == 0)
    def _():
        positions = lax.broadcasted_iota(jnp.int32, (rows, 128), 0)
        ids_ref[:rows, :] = ids(positions + own)
        ids_ref[rows:, :] = ids(positions + other)

    for step in range(count):

        @pl.when(head == step)
        def _():
            for index, source in enumerate(sources):
                fetch(step, source, index).wait()

    ko_ref, q_ref, vo_ref, g_ref = (held_ref.at[head, index] for index in range(4))
    k = jnp.concatenate([ko_ref[...], kp_ref[...]], 0)
    v = jnp.concatenate([vo_ref[...], vp_ref[...]], 0)
    k_t, v_t = k.T, v.T
    for i in range(rows // tile):
        part = slice(i * tile, (i + 1) * tile)
        q, g = q_ref[part, :], g_ref[part, :]
        query_ids = ids(lax.broadcasted_iota(jnp.int32, (8, tile), 1) + (own + i * tile))[:1]
        key_ids = jnp.concatenate([ids_ref[...]] * (tile // 128), 1)
        scores = jnp.where(key_ids == query_ids, dot_on(k, q, 1, 1) * to_exp2, NEG_FILL)
        peak = jnp.max(scores, axis=0, keepdims=True)
        raised = jnp.exp2(scores - peak)
        weights = raised * (1.0 / jnp.sum(raised, axis=0, keepdims=True))
        prob = weights.astype(BF16)
        att_t = dot_on(v_t, prob, 1, 0).astype(BF16).astype(F32)
        att_ref[part, :] = att_t.T.astype(BF16)
        delta = jnp.sum(g.astype(F32).T * att_t, axis=0, keepdims=True)
        grad_probs = dot_on(v, g, 1, 1)
        grad_scores = (weights * ((grad_probs - delta) * inverse)).astype(BF16)
        dq_ref[part, :] = dot_on(k_t, grad_scores, 1, 0).T.astype(BF16)
        dk = dot_on(grad_scores, q, 1, 0)
        dv = dot_on(prob, g, 1, 0)
        if i == 0:
            dk_acc[...] = dk
            dv_acc[...] = dv
        else:
            dk_acc[...] += dk
            dv_acc[...] += dv
    dko_ref[...] = dk_acc[:rows].astype(BF16)
    dkp_ref[...] = dk_acc[rows:].astype(BF16)
    dvo_ref[...] = dv_acc[:rows].astype(BF16)
    dvp_ref[...] = dv_acc[rows:].astype(BF16)


def cost(microseconds):
    return pl.CostEstimate(
        flops=int(microseconds * 1.15e9), bytes_accessed=0, transcendentals=0
    )


def attention(place, q, ko, kp, vo, vp, g, first, count, held, after):
    rows, width = q.shape
    spec = pl.BlockSpec((rows, HEAD_DIM), lambda i, *_: (0, i + first))
    return pl.pallas_call(
        functools.partial(attention_kernel, tile=256, first=first, count=count),
        grid_spec=pltpu.PrefetchScalarGridSpec(
            num_scalar_prefetch=1,
            grid=(count,),
            in_specs=[spec] * 2
            + [pl.BlockSpec(memory_space=pltpu.HBM)] * 4
            + [pl.BlockSpec(memory_space=pl.ANY)] * (len(held) + len(after)),
            out_specs=[spec] * 6 + [TOKEN_SPEC],
            scratch_shapes=[
                pltpu.VMEM((2 * rows, 128), jnp.int32),
                pltpu.VMEM((2 * rows, HEAD_DIM), F32),
                pltpu.VMEM((2 * rows, HEAD_DIM), F32),
                pltpu.VMEM((count, 4, rows, HEAD_DIM), BF16),
                pltpu.SemaphoreType.DMA((count, 4)),
            ],
        ),
        out_shape=[jax.ShapeDtypeStruct((rows, width), BF16)] * 6 + [TOKEN],
        input_output_aliases={7 + i: i for i in range(len(held))},
        compiler_params=pltpu.CompilerParams(vmem_limit_bytes=24 * MIB),
        cost_estimate=cost(0.2),
        name="attention",
    )(place, kp, vp, q, ko, vo, g, *held, *after)


def gate_kernel(*refs):
    pass


def gate(arrays, after):
    anywhere = pl.BlockSpec(memory_space=pl.ANY)
    return pl.pallas_call(
        gate_kernel,
        in_specs=[anywhere] * (len(arrays) + len(after)),
        out_specs=[anywhere] * len(arrays),
        out_shape=[jax.ShapeDtypeStruct(a.shape, a.dtype) for a in arrays],
        input_output_aliases={i: i for i in range(len(arrays))},
        compiler_params=pltpu.CompilerParams(vmem_limit_bytes=2 * MIB),
        cost_estimate=cost(0.0001),
        name="gate",
    )(*arrays, *after)


def half_kernel(whole_ref, half_ref, *, start):
    half_ref[...] = whole_ref[pl.ds(start, half_ref.shape[0]), :]


def half_of(array, second):
    rows, width = array.shape
    whole = pl.BlockSpec(memory_space=pltpu.VMEM)
    return pl.pallas_call(
        functools.partial(half_kernel, start=rows // 2 * second),
        in_specs=[whole],
        out_specs=whole,
        out_shape=jax.ShapeDtypeStruct((rows // 2, width), array.dtype),
        compiler_params=pltpu.CompilerParams(vmem_limit_bytes=4 * MIB),
        cost_estimate=cost(0.0001),
        name="half_of",
    )(array)


def origin(place_ref, pair, chips):
    return lax.rem(place_ref[1] + (chips - pair), chips)


def owns(place_ref, pair, chips):
    return (lax.div(origin(place_ref, pair, chips), chips // 2) == place_ref[0]).astype(jnp.int32)


def spot(place_ref, pair, chips):
    return lax.rem(origin(place_ref, pair, chips), chips // 2)


def pick_kernel(place_ref, near_ref, *refs, pair, chips, count):
    far_refs, out_ref = refs[:count], refs[-1]
    keep = owns(place_ref, pair, chips) == 1
    rows = near_ref.shape[0] // len(far_refs)
    for index, far_ref in enumerate(far_refs):
        part = slice(index * rows, (index + 1) * rows)
        out_ref[part, :] = jnp.where(keep, far_ref[...], near_ref[part, :])


def pick_other(place, near, far, pair, chips, after):
    rows, width = near.shape
    whole = pl.BlockSpec(memory_space=pltpu.VMEM)
    return pl.pallas_call(
        functools.partial(pick_kernel, pair=pair, chips=chips, count=len(far)),
        in_specs=[pl.BlockSpec(memory_space=pltpu.SMEM)]
        + [whole] * (1 + len(far))
        + [pl.BlockSpec(memory_space=pl.ANY)] * len(after),
        out_specs=whole,
        out_shape=jax.ShapeDtypeStruct((rows, width), near.dtype),
        compiler_params=pltpu.CompilerParams(vmem_limit_bytes=8 * MIB),
        cost_estimate=cost(0.0001),
        name="pick_other",
    )(place, near, *far, *after)


def weight_kernel(place_ref, *refs, pairs, pieces, chips, dp_count, after):
    near, refs = refs[: len(pairs)], refs[len(pairs) :]
    recv, refs = refs[: len(pairs)], refs[len(pairs) :]
    far, refs = refs[: len(pairs) * pieces], refs[len(pairs) * pieces :]
    atts, carried_hbm = refs[:2], refs[2]
    *known_refs, out_ref, peak_ref, carried_ref, sems = refs[3 + after :]
    step = pl.program_id(0)

    def fetch(index):
        block = 2 * spot(place_ref, pairs[index // 2], chips) + index % 2
        return pltpu.make_async_copy(carried_hbm.at[block], carried_ref.at[index], sems.at[index])

    @pl.when(step == 0)
    def _():
        for index in range(2 * len(pairs)):
            fetch(index).start()

    rows = near[0].shape[0]

    def chunk(side, part, piece):
        found = None
        for index, pair in enumerate(pairs):
            if side:
                value = recv[index][part, :]
            else:
                keep = owns(place_ref, pair, chips) == 1
                value = jnp.where(keep, near[index][part, :], far[index * pieces + piece][...])
            found = value if index == 0 else jnp.where(step < 2 * index, found, value)
        return found

    corrected = None
    for side in range(2):
        for piece in range(pieces):
            part = slice(piece * rows // pieces, (piece + 1) * rows // pieces)
            product = dot_on(chunk(side, part, piece), atts[side][part, :], 0, 0)
            corrected = product if corrected is None else corrected + product
    for index in range(2 * len(pairs)):

        @pl.when(step == index)
        def _():
            fetch(index).wait()

    corrected = corrected + carried_ref[step]
    share = corrected.shape[0] // dp_count
    peak_ref[pl.ds(step, 1), :] = jnp.max(jnp.abs(corrected), axis=0, keepdims=True)
    rounded = corrected.astype(BF16)
    place = pl.ds(pl.multiple_of(step * share, share), share)
    for dest in range(dp_count):
        out_ref[dest, place, :] = rounded[dest * share : (dest + 1) * share]
    if known_refs:

        @pl.when(step == 2 * len(pairs) - 1)
        def _():
            peaks = jnp.concatenate([peak_ref[...]] + [ref[...] for ref in known_refs], 0)
            high = peaks.astype(BF16).astype(F32)
            both = jnp.concatenate([high, peaks - high], 0).astype(BF16)
            for dest in range(dp_count):
                out_ref[dest, 2 * len(pairs) * share :, :] = both


def weight_block(
    place, near, far, recv, att, carried, known, pairs, chips, dp_count, after
):
    rows, width = att[0].shape
    block = carried.shape[1]
    share = block // dp_count
    count = len(pairs)
    pieces = len(far[0])
    out_rows = 2 * count * share + (16 if known else 0)
    whole = lambda i, *_: (0, 0)

    def column(index, wanted):
        def find(i, ref):
            return 0, jnp.clip(i - 2 * index, 0, 1) * wanted(owns(ref, pairs[index], chips))

        return find

    near_specs = [pl.BlockSpec((rows, block), column(n, lambda own: own)) for n in range(count)]
    recv_specs = [pl.BlockSpec((rows, block), column(n, lambda own: 1)) for n in range(count)]
    far_specs = [
        pl.BlockSpec((rows // pieces, block), column(n, lambda own: 1 - own))
        for n in range(count)
        for _ in range(pieces)
    ]
    return pl.pallas_call(
        functools.partial(
            weight_kernel,
            pairs=pairs,
            pieces=pieces,
            chips=chips,
            dp_count=dp_count,
            after=len(after),
        ),
        grid_spec=pltpu.PrefetchScalarGridSpec(
            num_scalar_prefetch=1,
            grid=(2 * count,),
            in_specs=near_specs
            + recv_specs
            + far_specs
            + [pl.BlockSpec((rows, width), whole)] * 2
            + [pl.BlockSpec(memory_space=pltpu.HBM)]
            + [pl.BlockSpec(memory_space=pl.ANY)] * len(after)
            + [pl.BlockSpec(array.shape, whole) for array in known],
            out_specs=[
                pl.BlockSpec((dp_count, out_rows, width), lambda i, *_: (0, 0, 0)),
                pl.BlockSpec((2 * count, width), whole),
            ],
            scratch_shapes=[
                pltpu.VMEM((2 * count, block, width), F32),
                pltpu.SemaphoreType.DMA((2 * count,)),
            ],
        ),
        out_shape=[
            jax.ShapeDtypeStruct((dp_count, out_rows, width), BF16),
            jax.ShapeDtypeStruct((2 * count, width), F32),
        ],
        compiler_params=pltpu.CompilerParams(vmem_limit_bytes=28 * MIB),
        cost_estimate=cost(0.0001),
        name="weight_block",
    )(place, *near, *recv, *[p for f in far for p in f], *att, carried, *after, *known)


def add_kernel(a_ref, b_ref, c_ref, d_ref, first_ref, second_ref):
    first_ref[...] = (a_ref[...].astype(F32) + b_ref[...].astype(F32)).astype(BF16)
    second_ref[...] = (c_ref[...].astype(F32) + d_ref[...].astype(F32)).astype(BF16)


def add_pairs(a, b, c, d):
    rows, width = a.shape
    spec = pl.BlockSpec((rows // 4, width), lambda i: (i, 0))
    return pl.pallas_call(
        add_kernel,
        grid=(4,),
        in_specs=[spec] * 4,
        out_specs=[spec] * 2,
        out_shape=[jax.ShapeDtypeStruct((rows, width), BF16)] * 2,
        compiler_params=pltpu.CompilerParams(vmem_limit_bytes=8 * MIB),
        cost_estimate=cost(0.0001),
        name="add_pairs",
    )(a, b, c, d)


def finish_kernel(place_ref, last_ref, sides_ref, middle_ref, levels_ref, scale_ref, *, chips):
    share = levels_ref.shape[1]
    head = 2 * share
    peaks = jnp.max(
        last_ref[:, head : head + 8, :].astype(F32) + last_ref[:, head + 8 : head + 16, :].astype(F32),
        axis=0,
    )
    scale = (peaks + 1e-6) / 7.0
    for index, pair in enumerate((0, 1, 3, 2)):
        for half in range(2):
            block = 2 * spot(place_ref, pair, chips) + half
            row = scale[2 * index + half : 2 * index + half + 1]
            scale_ref[pl.ds(block, 1), :] = row
            terms_ref = (last_ref, sides_ref, sides_ref, middle_ref)[index]
            start = ((pair == 3) * 2 + half) * share
            terms = terms_ref[pl.ds(start, share), :] if index else jnp.sum(
                terms_ref[:, start : start + share, :].astype(F32), axis=0
            )
            levels_ref[block] = terms / row


def finish(place, last, sides, middle, share, chips):
    width = last.shape[2]
    vmem = pl.BlockSpec(memory_space=pltpu.VMEM)
    return pl.pallas_call(
        functools.partial(finish_kernel, chips=chips),
        in_specs=[pl.BlockSpec(memory_space=pltpu.SMEM)] + [vmem] * 3,
        out_specs=[vmem] * 2,
        out_shape=[
            jax.ShapeDtypeStruct((8, share, width), F32),
            jax.ShapeDtypeStruct((8, width), F32),
        ],
        compiler_params=pltpu.CompilerParams(vmem_limit_bytes=12 * MIB),
        cost_estimate=cost(0.0001),
        name="finish",
    )(place, last, sides, middle)


def body(query_in, key_in, value_in, attn_grad, out_grad, carried_error, lengths):
    dp_count = lax.axis_size("dp")
    z_count = lax.axis_size("tensor")
    seq = lax.axis_index("seq")
    z = lax.axis_index("tensor")
    up = [(i, (i + 1) % z_count) for i in range(z_count)]
    down = [(i, (i - 1) % z_count) for i in range(z_count)]
    swap = [(0, 1), (1, 0)]

    def peer(array):
        return lax.ppermute(array, "seq", swap)

    own = out_grad[0]
    place = jnp.concatenate([jnp.stack([seq, z]).astype(jnp.int32), lengths[0]])
    heads = own.shape[1] // HEAD_DIM

    def send_up(array):
        return lax.ppermute(array, "tensor", up)

    def send_down(array):
        return lax.ppermute(array, "tensor", down)

    def stay(array):
        return pltpu.with_memory_space_constraint(array, pltpu.HBM)

    from_down, from_up = {1: send_up(own)}, {1: send_down(own)}
    tokens = (
        stay(query_in[0]),
        stay(key_in[0]),
        peer(key_in[0]),
        stay(value_in[0]),
        peer(value_in[0]),
        stay(attn_grad[0]),
    )
    carried = stay(carried_error[0])
    *held, token = attention(place, *tokens, 0, heads // 2, [], [])
    (from_down[1],) = gate([from_down[1]], [token])
    from_down[2] = send_up(from_down[1])
    (from_up[1],) = gate([from_up[1]], [token])
    from_up[2] = send_down(from_up[1])
    att, dq, dk_own, dk_peer, dv_own, dv_peer, token = attention(
        place, *tokens, heads // 2, heads // 2, held, [from_down[1], from_up[1]]
    )
    from_down[2], att = gate([from_down[2], att], [token])
    from_down[3] = send_up(from_down[2])
    (from_up[2],) = gate([from_up[2]], [token])
    from_up[3] = send_down(from_up[2])
    atts = (att, peer(att))
    share = carried.shape[1] // dp_count

    def swapped(pair, near, far, after=()):
        return peer(pick_other(place, near, far, pair, z_count, after))

    def weigh(pairs, near, far, recv, known=(), after=()):
        return weight_block(
            place, near, far, recv, atts, carried, known, pairs, z_count, dp_count, after
        )

    def exchange(array):
        return lax.all_to_all(array, "dp", 0, 0, tiled=True)

    recv2 = swapped(2, from_down[2], [from_up[2]])
    terms, peaks2 = weigh((2,), [from_down[2]], [[from_up[2]]], [recv2])
    middle = jnp.sum(exchange(terms).astype(F32), axis=0)
    (from_down[3],) = gate([from_down[3]], [peaks2])
    farthest = [send_up(half_of(from_down[3], 0))]
    (from_up[3],) = gate([from_up[3]], [peaks2])
    farthest.append(send_down(half_of(from_up[3], 1)))
    recv1 = swapped(1, from_down[1], [from_up[3]])
    recv3 = swapped(3, from_down[3], [from_up[1]])
    terms, peaks13 = weigh(
        (1, 3),
        [from_down[1], from_down[3]],
        [[from_up[3]], [from_up[1]]],
        [recv1, recv3],
    )
    *farthest, terms = gate([*farthest, terms], [peaks13, middle])
    sides = exchange(terms)
    recv0 = swapped(0, own, farthest)
    terms, _ = weigh((0,), [own], [farthest], [recv0], (peaks13, peaks2))
    last = exchange(terms)
    d_keys, d_values = add_pairs(dk_own, peer(dk_peer), dv_own, peer(dv_peer))
    level_sums, block_scale = finish(
        place,
        last,
        jnp.sum(sides.astype(F32), axis=0),
        middle,
        share,
        z_count,
    )
    return dq[None], d_keys[None], d_values[None], level_sums, block_scale


def solution(mesh):
    tokens = P("dp", "seq", "tensor")
    in_specs = (tokens,) * 5 + (P("dp", "seq", None, "tensor"), P("dp", None))
    out_specs = (tokens,) * 3 + (P("seq", "dp", "tensor"), P("seq", "tensor"))
    return jax.shard_map(body, mesh=mesh, in_specs=in_specs, out_specs=out_specs, check_vma=False)
```

```python
import functools
import math

import jax
import jax.numpy as jnp
from jax import lax
from jax.experimental import pallas as pl
from jax.experimental.pallas import tpu as pltpu
from jax.sharding import PartitionSpec as P

HEAD_DIM = 128
NEG_FILL = -1e30
F32 = jnp.float32
BF16 = jnp.bfloat16
MIB = 2**20
LANES = 128
TOKEN = jax.ShapeDtypeStruct((8, 128), F32)
TOKEN_SPEC = pl.BlockSpec((8, 128), lambda i, *_: (0, 0))


def dot_on(a, b, a_dim, b_dim):
    return lax.dot_general(a, b, (((a_dim,), (b_dim,)), ((), ())), preferred_element_type=F32)


def attention_kernel(
    place_ref, kp_ref, vp_ref, q_hbm, ko_hbm, vo_hbm, g_hbm, *refs, tile, first, count
):
    att_ref, dq_ref, dko_ref, dkp_ref, dvo_ref, dvp_ref, token_ref = refs[-12:-5]
    ids_ref, dk_acc, dv_acc, held_ref, sems = refs[-5:]
    token_ref[...] = jnp.zeros_like(token_ref)
    rows = kp_ref.shape[0]
    head = pl.program_id(0)

    def fetch(step, source, index):
        column = pl.ds((first + step) * HEAD_DIM, HEAD_DIM)
        return pltpu.make_async_copy(
            source.at[:, column], held_ref.at[step, index], sems.at[step, index]
        )

    sources = (ko_hbm, q_hbm, vo_hbm, g_hbm)

    @pl.when(head == 0)
    def _():
        for step in range(count):
            for index, source in enumerate(sources):
                fetch(step, source, index).start()
    inverse = 1.0 / math.sqrt(HEAD_DIM)
    to_exp2 = inverse * math.log2(math.e)
    own = place_ref[0] * rows
    other = rows - own

    def ids(positions):
        found = jnp.zeros(positions.shape, jnp.int32)
        end = jnp.int32(0)
        for image in range(4):
            end = end + place_ref[2 + image]
            found = found + (positions >= end).astype(jnp.int32)
        return found

    @pl.when(head == 0)
    def _():
        positions = lax.broadcasted_iota(jnp.int32, (rows, 128), 0)
        ids_ref[:rows, :] = ids(positions + own)
        ids_ref[rows:, :] = ids(positions + other)

    for step in range(count):

        @pl.when(head == step)
        def _():
            for index, source in enumerate(sources):
                fetch(step, source, index).wait()

    ko_ref, q_ref, vo_ref, g_ref = (held_ref.at[head, index] for index in range(4))
    k = jnp.concatenate([ko_ref[...], kp_ref[...]], 0)
    v = jnp.concatenate([vo_ref[...], vp_ref[...]], 0)
    k_t, v_t = k.T, v.T
    for i in range(rows // tile):
        part = slice(i * tile, (i + 1) * tile)
        q, g = q_ref[part, :], g_ref[part, :]
        query_ids = ids(lax.broadcasted_iota(jnp.int32, (8, tile), 1) + (own + i * tile))[:1]
        key_ids = jnp.concatenate([ids_ref[...]] * (tile // 128), 1)
        scores = jnp.where(key_ids == query_ids, dot_on(k, q, 1, 1) * to_exp2, NEG_FILL)
        peak = jnp.max(scores, axis=0, keepdims=True)
        raised = jnp.exp2(scores - peak)
        weights = raised * (1.0 / jnp.sum(raised, axis=0, keepdims=True))
        prob = weights.astype(BF16)
        att_t = dot_on(v_t, prob, 1, 0).astype(BF16).astype(F32)
        att_ref[part, :] = att_t.T.astype(BF16)
        delta = jnp.sum(g.astype(F32).T * att_t, axis=0, keepdims=True)
        grad_probs = dot_on(v, g, 1, 1)
        grad_scores = (weights * ((grad_probs - delta) * inverse)).astype(BF16)
        dq_ref[part, :] = dot_on(k_t, grad_scores, 1, 0).T.astype(BF16)
        dk = dot_on(grad_scores, q, 1, 0)
        dv = dot_on(prob, g, 1, 0)
        if i == 0:
            dk_acc[...] = dk
            dv_acc[...] = dv
        else:
            dk_acc[...] += dk
            dv_acc[...] += dv
    dko_ref[...] = dk_acc[:rows].astype(BF16)
    dkp_ref[...] = dk_acc[rows:].astype(BF16)
    dvo_ref[...] = dv_acc[:rows].astype(BF16)
    dvp_ref[...] = dv_acc[rows:].astype(BF16)


def cost(microseconds, *arrays):
    size = sum(array.size * array.dtype.itemsize for array in arrays)
    return pl.CostEstimate(
        flops=int(microseconds * 1.15e9), bytes_accessed=size, transcendentals=0
    )


def attention(place, q, ko, kp, vo, vp, g, first, count, held, after):
    rows, width = q.shape
    spec = pl.BlockSpec((rows, HEAD_DIM), lambda i, *_: (0, i + first))
    return pl.pallas_call(
        functools.partial(attention_kernel, tile=256, first=first, count=count),
        grid_spec=pltpu.PrefetchScalarGridSpec(
            num_scalar_prefetch=1,
            grid=(count,),
            in_specs=[spec] * 2
            + [pl.BlockSpec(memory_space=pltpu.HBM)] * 4
            + [pl.BlockSpec(memory_space=pl.ANY)] * (len(held) + len(after)),
            out_specs=[spec] * 6 + [TOKEN_SPEC],
            scratch_shapes=[
                pltpu.VMEM((2 * rows, 128), jnp.int32),
                pltpu.VMEM((2 * rows, HEAD_DIM), F32),
                pltpu.VMEM((2 * rows, HEAD_DIM), F32),
                pltpu.VMEM((count, 4, rows, HEAD_DIM), BF16),
                pltpu.SemaphoreType.DMA((count, 4)),
            ],
        ),
        out_shape=[pltpu.VMEM((rows, width), BF16)]
        + [pltpu.HBM((rows, width), BF16)] * 5
        + [TOKEN],
        input_output_aliases={7 + i: i for i in range(len(held))},
        compiler_params=pltpu.CompilerParams(vmem_limit_bytes=18 * MIB),
        cost_estimate=cost(0.2),
        name="attention",
    )(place, kp, vp, q, ko, vo, g, *held, *after)


def gate_kernel(*refs):
    pass


def gate(arrays, after, microseconds=0.01, space=jax.ShapeDtypeStruct):
    anywhere = pl.BlockSpec(memory_space=pl.ANY)
    return pl.pallas_call(
        gate_kernel,
        in_specs=[anywhere] * (len(arrays) + len(after)),
        out_specs=[anywhere] * len(arrays),
        out_shape=[space(a.shape, a.dtype) for a in arrays],
        input_output_aliases={i: i for i in range(len(arrays))},
        compiler_params=pltpu.CompilerParams(vmem_limit_bytes=2 * MIB),
        cost_estimate=cost(microseconds),
        name="gate",
    )(*arrays, *after)


def origin(place_ref, pair, chips):
    return lax.rem(place_ref[1] + (chips - pair), chips)


def owns(place_ref, pair, chips):
    return (lax.div(origin(place_ref, pair, chips), chips // 2) == place_ref[0]).astype(jnp.int32)


def spot(place_ref, pair, chips):
    return lax.rem(origin(place_ref, pair, chips), chips // 2)


def pick_kernel(place_ref, near_ref, *refs, pair, chips, count):
    far_refs, out_ref = refs[:count], refs[-1]
    keep = owns(place_ref, pair, chips) == 1
    rows = near_ref.shape[0] // len(far_refs)
    for index, far_ref in enumerate(far_refs):
        part = slice(index * rows, (index + 1) * rows)
        out_ref[part, :] = jnp.where(keep, far_ref[...], near_ref[part, :])


def pick_other(place, near, far, pair, chips, after):
    rows, width = near.shape
    whole = pl.BlockSpec(memory_space=pltpu.VMEM)
    return pl.pallas_call(
        functools.partial(pick_kernel, pair=pair, chips=chips, count=len(far)),
        in_specs=[pl.BlockSpec(memory_space=pltpu.SMEM)]
        + [whole] * (1 + len(far))
        + [pl.BlockSpec(memory_space=pl.ANY)] * len(after),
        out_specs=whole,
        out_shape=pltpu.VMEM((rows, width), near.dtype),
        compiler_params=pltpu.CompilerParams(vmem_limit_bytes=4 * MIB),
        cost_estimate=cost(0.01),
        name="pick_other",
    )(place, near, *far, *after)


def fork_kernel(place_ref, down_ref, up_ref, old_down_ref, old_up_ref, *out_refs, chips):
    top_ref, bottom_ref, first_ref, third_ref = out_refs
    half = top_ref.shape[0]
    top_ref[...] = down_ref[:half, :]
    bottom_ref[...] = up_ref[half:, :]
    first_ref[...] = jnp.where(
        owns(place_ref, 1, chips) == 1, up_ref[...], old_down_ref[...]
    )
    third_ref[...] = jnp.where(
        owns(place_ref, 3, chips) == 1, old_up_ref[...], down_ref[...]
    )


def fork(place, down, up, old_down, old_up, chips):
    rows, width = down.shape
    vmem = pl.BlockSpec(memory_space=pltpu.VMEM)
    return pl.pallas_call(
        functools.partial(fork_kernel, chips=chips),
        in_specs=[pl.BlockSpec(memory_space=pltpu.SMEM)] + [vmem] * 4,
        out_specs=[vmem] * 4,
        out_shape=[jax.ShapeDtypeStruct((rows // 2, width), down.dtype)] * 2
        + [jax.ShapeDtypeStruct((rows, width), down.dtype)] * 2,
        compiler_params=pltpu.CompilerParams(vmem_limit_bytes=6 * MIB),
        cost_estimate=cost(0.01),
        name="fork",
    )(place, down, up, old_down, old_up)


def weight_kernel(place_ref, *refs, pairs, pieces, chips, dp_count, known, keep_att):
    count = len(pairs)
    near, refs = refs[:count], refs[count:]
    recv, refs = refs[:count], refs[count:]
    far, refs = refs[: count * pieces], refs[count * pieces :]
    att_refs, carried_ref, refs = refs[:2], refs[2], refs[3:]
    known_refs, refs = refs[:known], refs[known:]
    out_ref, peak_ref, *kept_refs, atts, mine, other, carried, terms, sems, out_sems = refs
    rows, width = att_refs[0].shape
    block = carried.shape[1]
    share = block // dp_count
    part_rows = rows // pieces
    groups = width // LANES
    peak_rows = 8 * groups

    def part(piece):
        return slice(piece * part_rows, (piece + 1) * part_rows)

    def fetch_mine(index, piece, from_near):
        source = near[index].at[part(piece)] if from_near else far[index * pieces + piece]
        return pltpu.make_async_copy(source, mine.at[index, part(piece)], sems.at[1 + piece, index])

    def fetch_other(index):
        return pltpu.make_async_copy(recv[index], other.at[index], sems.at[0, index])

    def fetch_att(side):
        return pltpu.make_async_copy(att_refs[side], atts.at[side], sems.at[3, side])

    def fetch_carried(index):
        place = 2 * spot(place_ref, pairs[index // 2], chips) + index % 2
        return pltpu.make_async_copy(carried_ref.at[place], carried.at[index], sems.at[4, index])

    def send(index):
        if known:
            place = pl.ds(index * groups * share, groups * share if index < 2 * count else peak_rows)
            return pltpu.make_async_copy(
                terms.at[:, place], out_ref.at[:, place], out_sems.at[index]
            )
        place = pl.ds(index * share, share)
        return pltpu.make_async_copy(terms.at[index], out_ref.at[:, place], out_sems.at[index])

    def keep_copy():
        return pltpu.make_async_copy(atts.at[1], kept_refs[0], out_sems.at[2 * count])

    fetch_att(0).start()
    for index, pair in enumerate(pairs):
        keep = owns(place_ref, pair, chips) == 1
        for piece in range(pieces):
            pl.when(keep)(fetch_mine(index, piece, True).start)
            pl.when(jnp.logical_not(keep))(fetch_mine(index, piece, False).start)
        fetch_other(index).start()
        if index == 0:
            fetch_att(1).start()
        fetch_carried(2 * index).start()
        fetch_carried(2 * index + 1).start()
    fetch_att(0).wait()
    for index in range(count):
        for piece in range(pieces):
            fetch_mine(index, piece, True).wait()
        for half in range(2):
            columns = slice(half * block, (half + 1) * block)
            corrected = dot_on(mine[index, :, columns], atts[0], 0, 0)
            if half == 0:
                fetch_other(index).wait()
                if index == 0:
                    fetch_att(1).wait()
                    if keep_att:
                        keep_copy().start()
            corrected = corrected + dot_on(other[index, :, columns], atts[1], 0, 0)
            slot = 2 * index + half
            fetch_carried(slot).wait()
            corrected = corrected + carried[slot]
            peak_ref[slot : slot + 1, :] = jnp.max(jnp.abs(corrected), axis=0, keepdims=True)
            rounded = corrected.astype(BF16).reshape(dp_count, share, width)
            if known:
                for group in range(groups):
                    row = (slot * groups + group) * share
                    lanes = slice(group * LANES, (group + 1) * LANES)
                    terms[:, row : row + share, :] = rounded[:, :, lanes]
            else:
                terms[slot] = rounded
            send(slot).start()
    slots = 2 * count
    if known:
        peaks = jnp.concatenate([peak_ref[...]] + [ref[...] for ref in known_refs], 0)
        peaks = jnp.concatenate(
            [peaks[:, group * LANES : (group + 1) * LANES] for group in range(groups)], 0
        ).astype(BF16)
        for dest in range(dp_count):
            terms[dest, slots * groups * share :, :] = peaks
        send(slots).start()
        slots += 1
    for slot in range(slots):
        send(slot).wait()
    if keep_att:
        keep_copy().wait()


def weight_block(place, near, far, recv, att, carried, known, pairs, chips, dp_count, keep_att):
    rows, width = att[0].shape
    block = carried.shape[1]
    share = block // dp_count
    count = len(pairs)
    pieces = len(far[0])
    if known:
        groups = width // LANES
        out_rows = 2 * count * groups * share + 8 * groups
        out_shape = pltpu.HBM((dp_count, out_rows, LANES), BF16)
        terms = pltpu.VMEM((dp_count, out_rows, LANES), BF16)
    else:
        out_shape = pltpu.HBM((dp_count, 2 * count * share, width), BF16)
        terms = pltpu.VMEM((2 * count, dp_count, share, width), BF16)
    vmem = pl.BlockSpec(memory_space=pltpu.VMEM)
    anywhere = pl.BlockSpec(memory_space=pl.ANY)
    hbm = pl.BlockSpec(memory_space=pltpu.HBM)
    return pl.pallas_call(
        functools.partial(
            weight_kernel,
            pairs=pairs,
            pieces=pieces,
            chips=chips,
            dp_count=dp_count,
            known=len(known),
            keep_att=keep_att,
        ),
        in_specs=[pl.BlockSpec(memory_space=pltpu.SMEM)]
        + [anywhere] * (count * (2 + pieces) + 2)
        + [hbm]
        + [vmem] * len(known),
        out_specs=[hbm, vmem] + [hbm] * keep_att,
        out_shape=[out_shape, jax.ShapeDtypeStruct((2 * count, width), F32)]
        + [pltpu.HBM((rows, width), BF16)] * keep_att,
        scratch_shapes=[
            pltpu.VMEM((2, rows, width), BF16),
            pltpu.VMEM((count, rows, 2 * block), BF16),
            pltpu.VMEM((count, rows, 2 * block), BF16),
            pltpu.VMEM((2 * count, block, width), F32),
            terms,
            pltpu.SemaphoreType.DMA((5, 2 * max(count, 1))),
            pltpu.SemaphoreType.DMA((2 * count + 1,)),
        ],
        compiler_params=pltpu.CompilerParams(vmem_limit_bytes=20 * MIB),
        cost_estimate=cost(0.1),
        name="weight_block",
    )(place, *near, *recv, *[p for f in far for p in f], *att, carried, *known)


def add_kernel(a_ref, b_ref, c_ref, d_ref, first_ref, second_ref):
    first_ref[...] = (a_ref[...].astype(F32) + b_ref[...].astype(F32)).astype(BF16)
    second_ref[...] = (c_ref[...].astype(F32) + d_ref[...].astype(F32)).astype(BF16)


def add_pairs(a, b, c, d):
    rows, width = a.shape
    spec = pl.BlockSpec((rows // 4, width), lambda i: (i, 0))
    return pl.pallas_call(
        add_kernel,
        grid=(4,),
        in_specs=[spec] * 4,
        out_specs=[spec] * 2,
        out_shape=[jax.ShapeDtypeStruct((rows, width), BF16)] * 2,
        compiler_params=pltpu.CompilerParams(vmem_limit_bytes=8 * MIB),
        cost_estimate=cost(0.1),
        name="add_pairs",
    )(a, b, c, d)


def finish_kernel(place_ref, last_ref, sides_ref, middle_ref, levels_ref, scale_ref, *, chips):
    share, width = levels_ref.shape[1:]
    groups = width // LANES
    rows = 2 * groups * share
    total = jnp.sum(last_ref[:, :rows, :].astype(F32), axis=0)
    peaks = jnp.max(last_ref[:, rows:, :].astype(F32), axis=0)
    scale = jnp.concatenate([peaks[group * 8 : group * 8 + 8] for group in range(groups)], 1)
    scale = (scale + 1e-6) / 7.0
    for index, pair in enumerate((0, 1, 3, 2)):
        for half in range(2):
            block = 2 * spot(place_ref, pair, chips) + half
            row = scale[2 * index + half : 2 * index + half + 1]
            scale_ref[pl.ds(block, 1), :] = row
            if pair == 0:
                pieces = [
                    total[(half * groups + group) * share : (half * groups + group + 1) * share]
                    for group in range(groups)
                ]
                terms = jnp.concatenate(pieces, 1)
            else:
                terms_ref = middle_ref if pair == 2 else sides_ref
                start = ((pair == 3) * 2 + half) * share
                terms = terms_ref[pl.ds(start, share), :]
            levels_ref[block] = terms / row


def finish(place, last, sides, middle, share, chips):
    width = middle.shape[1]
    vmem = pl.BlockSpec(memory_space=pltpu.VMEM)
    return pl.pallas_call(
        functools.partial(finish_kernel, chips=chips),
        in_specs=[pl.BlockSpec(memory_space=pltpu.SMEM)] + [vmem] * 3,
        out_specs=[vmem] * 2,
        out_shape=[
            jax.ShapeDtypeStruct((8, share, width), F32),
            jax.ShapeDtypeStruct((8, width), F32),
        ],
        compiler_params=pltpu.CompilerParams(vmem_limit_bytes=12 * MIB),
        cost_estimate=cost(0.1),
        name="finish",
    )(place, last, sides, middle)


def body(query_in, key_in, value_in, attn_grad, out_grad, carried_error, lengths):
    dp_count = lax.axis_size("dp")
    z_count = lax.axis_size("tensor")
    seq = lax.axis_index("seq")
    z = lax.axis_index("tensor")
    up = [(i, (i + 1) % z_count) for i in range(z_count)]
    down = [(i, (i - 1) % z_count) for i in range(z_count)]
    swap = [(0, 1), (1, 0)]

    def peer(array):
        return lax.ppermute(array, "seq", swap)

    own = out_grad[0]
    place = jnp.concatenate([jnp.stack([seq, z]).astype(jnp.int32), lengths[0]])
    heads = own.shape[1] // HEAD_DIM

    def send_up(array):
        return lax.ppermute(array, "tensor", up)

    def send_down(array):
        return lax.ppermute(array, "tensor", down)

    def stay(array):
        return pltpu.with_memory_space_constraint(array, pltpu.HBM)

    from_down, from_up = {1: send_up(own)}, {1: send_down(own)}
    tokens = (
        stay(query_in[0]),
        stay(key_in[0]),
        peer(key_in[0]),
        stay(value_in[0]),
        peer(value_in[0]),
        stay(attn_grad[0]),
    )
    carried = stay(carried_error[0])
    *held, token = attention(place, *tokens, 0, heads // 2, [], [])
    (from_down[1],) = gate([from_down[1]], [token])
    from_down[2] = send_up(from_down[1])
    (from_up[1],) = gate([from_up[1]], [token])
    from_up[2] = send_down(from_up[1])
    att, dq, dk_own, dk_peer, dv_own, dv_peer, token = attention(
        place, *tokens, heads // 2, heads // 2, held, [from_down[1], from_up[1]]
    )
    from_down[2], att = gate([from_down[2], att], [token])
    from_down[3] = send_up(from_down[2])
    (from_up[2],) = gate([from_up[2]], [token])
    from_up[3] = send_down(from_up[2])
    share = carried.shape[1] // dp_count

    def swapped(pair, near, far, after=()):
        return peer(pick_other(place, near, far, pair, z_count, after))

    def weigh(pairs, near, far, recv, atts, known=(), keep_att=False):
        return weight_block(
            place, near, far, recv, atts, carried, known, pairs, z_count, dp_count, keep_att
        )

    def exchange(array):
        return lax.all_to_all(array, "dp", 0, 0, tiled=True)

    recv2 = swapped(2, from_down[2], [from_up[2]])
    terms, peaks2, att_peer = weigh(
        (2,), [from_down[2]], [[from_up[2]]], [recv2], (att, peer(att)), keep_att=True
    )
    atts = (att, stay(att_peer))
    (middle,) = gate([exchange(terms)], [], 6.0)
    from_down[3], from_up[3] = gate([from_down[3], from_up[3]], [peaks2])
    top, bottom, send1, send3 = fork(
        place, from_down[3], from_up[3], from_down[1], from_up[1], z_count
    )
    farthest = [send_up(top), send_down(bottom)]
    terms, peaks13 = weigh(
        (1, 3),
        [from_down[1], from_down[3]],
        [[from_up[3]], [from_up[1]]],
        [peer(send1), peer(send3)],
        atts,
    )
    farthest = gate(farthest, [peaks13, middle])
    (terms,) = gate([terms], farthest, space=pltpu.HBM)
    (sides,) = gate([exchange(terms)], [])
    recv0 = swapped(0, own, farthest)
    terms, _ = weigh((0,), [own], [farthest], [recv0], atts, (peaks13, peaks2))
    last = exchange(terms)
    d_keys, d_values = add_pairs(dk_own, peer(dk_peer), dv_own, peer(dv_peer))
    level_sums, block_scale = finish(
        place,
        last,
        jnp.sum(sides.astype(F32), axis=0),
        jnp.sum(middle.astype(F32), axis=0),
        share,
        z_count,
    )
    return dq[None], d_keys[None], d_values[None], level_sums, block_scale


def solution(mesh):
    tokens = P("dp", "seq", "tensor")
    in_specs = (tokens,) * 5 + (P("dp", "seq", None, "tensor"), P("dp", None))
    out_specs = (tokens,) * 3 + (P("seq", "dp", "tensor"), P("seq", "tensor"))
    return jax.shard_map(body, mesh=mesh, in_specs=in_specs, out_specs=out_specs, check_vma=False)
```

```python
import functools
import math

import jax
import jax.numpy as jnp
from jax import lax
from jax.experimental import pallas as pl
from jax.experimental.pallas import tpu as pltpu
from jax.sharding import PartitionSpec as P

HEAD_DIM = 128
NEG_FILL = -1e30
F32 = jnp.float32
BF16 = jnp.bfloat16
MIB = 2**20
LANES = 128
TOKEN = jax.ShapeDtypeStruct((8, 128), F32)
TOKEN_SPEC = pl.BlockSpec((8, 128), lambda i, *_: (0, 0))


def dot_on(a, b, a_dim, b_dim):
    return lax.dot_general(a, b, (((a_dim,), (b_dim,)), ((), ())), preferred_element_type=F32)


def attention_kernel(
    place_ref, kp_ref, vp_ref, q_hbm, ko_hbm, vo_hbm, g_hbm, *refs, tile, first, count
):
    att_ref, dq_ref, dko_ref, dkp_ref, dvo_ref, dvp_ref, token_ref = refs[-12:-5]
    ids_ref, dk_acc, dv_acc, held_ref, sems = refs[-5:]
    token_ref[...] = jnp.zeros_like(token_ref)
    rows = kp_ref.shape[0]
    head = pl.program_id(0)

    def fetch(step, source, index):
        column = pl.ds((first + step) * HEAD_DIM, HEAD_DIM)
        return pltpu.make_async_copy(
            source.at[:, column], held_ref.at[step, index], sems.at[step, index]
        )

    sources = (ko_hbm, q_hbm, vo_hbm, g_hbm)

    @pl.when(head == 0)
    def _():
        for step in range(count):
            for index, source in enumerate(sources):
                fetch(step, source, index).start()
    inverse = 1.0 / math.sqrt(HEAD_DIM)
    to_exp2 = inverse * math.log2(math.e)
    own = place_ref[0] * rows
    other = rows - own

    def ids(positions):
        found = jnp.zeros(positions.shape, jnp.int32)
        end = jnp.int32(0)
        for image in range(4):
            end = end + place_ref[2 + image]
            found = found + (positions >= end).astype(jnp.int32)
        return found

    @pl.when(head == 0)
    def _():
        positions = lax.broadcasted_iota(jnp.int32, (rows, 128), 0)
        ids_ref[:rows, :] = ids(positions + own)
        ids_ref[rows:, :] = ids(positions + other)

    for step in range(count):

        @pl.when(head == step)
        def _():
            for index, source in enumerate(sources):
                fetch(step, source, index).wait()

    ko_ref, q_ref, vo_ref, g_ref = (held_ref.at[head, index] for index in range(4))
    k = jnp.concatenate([ko_ref[...], kp_ref[...]], 0)
    v = jnp.concatenate([vo_ref[...], vp_ref[...]], 0)
    k_t, v_t = k.T, v.T
    for i in range(rows // tile):
        part = slice(i * tile, (i + 1) * tile)
        q, g = q_ref[part, :], g_ref[part, :]
        query_ids = ids(lax.broadcasted_iota(jnp.int32, (8, tile), 1) + (own + i * tile))[:1]
        key_ids = jnp.concatenate([ids_ref[...]] * (tile // 128), 1)
        scores = jnp.where(key_ids == query_ids, dot_on(k, q, 1, 1) * to_exp2, NEG_FILL)
        peak = jnp.max(scores, axis=0, keepdims=True)
        raised = jnp.exp2(scores - peak)
        weights = raised * (1.0 / jnp.sum(raised, axis=0, keepdims=True))
        prob = weights.astype(BF16)
        att_t = dot_on(v_t, prob, 1, 0).astype(BF16).astype(F32)
        att_ref[part, :] = att_t.T.astype(BF16)
        delta = jnp.sum(g.astype(F32).T * att_t, axis=0, keepdims=True)
        grad_probs = dot_on(v, g, 1, 1)
        grad_scores = (weights * ((grad_probs - delta) * inverse)).astype(BF16)
        dq_ref[part, :] = dot_on(k_t, grad_scores, 1, 0).T.astype(BF16)
        dk = dot_on(grad_scores, q, 1, 0)
        dv = dot_on(prob, g, 1, 0)
        if i == 0:
            dk_acc[...] = dk
            dv_acc[...] = dv
        else:
            dk_acc[...] += dk
            dv_acc[...] += dv
    dko_ref[...] = dk_acc[:rows].astype(BF16)
    dkp_ref[...] = dk_acc[rows:].astype(BF16)
    dvo_ref[...] = dv_acc[:rows].astype(BF16)
    dvp_ref[...] = dv_acc[rows:].astype(BF16)


def cost(microseconds, *arrays):
    size = sum(array.size * array.dtype.itemsize for array in arrays)
    return pl.CostEstimate(
        flops=int(microseconds * 1.15e9), bytes_accessed=size, transcendentals=0
    )


def attention(place, q, ko, kp, vo, vp, g, first, count, held, after):
    rows, width = q.shape
    spec = pl.BlockSpec((rows, HEAD_DIM), lambda i, *_: (0, i + first))
    return pl.pallas_call(
        functools.partial(attention_kernel, tile=256, first=first, count=count),
        grid_spec=pltpu.PrefetchScalarGridSpec(
            num_scalar_prefetch=1,
            grid=(count,),
            in_specs=[spec] * 2
            + [pl.BlockSpec(memory_space=pltpu.HBM)] * 4
            + [pl.BlockSpec(memory_space=pl.ANY)] * (len(held) + len(after)),
            out_specs=[spec] * 6 + [TOKEN_SPEC],
            scratch_shapes=[
                pltpu.VMEM((2 * rows, 128), jnp.int32),
                pltpu.VMEM((2 * rows, HEAD_DIM), F32),
                pltpu.VMEM((2 * rows, HEAD_DIM), F32),
                pltpu.VMEM((count, 4, rows, HEAD_DIM), BF16),
                pltpu.SemaphoreType.DMA((count, 4)),
            ],
        ),
        out_shape=[pltpu.VMEM((rows, width), BF16)]
        + [pltpu.HBM((rows, width), BF16)] * 5
        + [TOKEN],
        input_output_aliases={7 + i: i for i in range(len(held))},
        compiler_params=pltpu.CompilerParams(vmem_limit_bytes=18 * MIB),
        cost_estimate=cost(0.2),
        name="attention",
    )(place, kp, vp, q, ko, vo, g, *held, *after)


def gate_kernel(*refs):
    pass


def gate(arrays, after, microseconds=0.01, space=jax.ShapeDtypeStruct):
    anywhere = pl.BlockSpec(memory_space=pl.ANY)
    return pl.pallas_call(
        gate_kernel,
        in_specs=[anywhere] * (len(arrays) + len(after)),
        out_specs=[anywhere] * len(arrays),
        out_shape=[space(a.shape, a.dtype) for a in arrays],
        input_output_aliases={i: i for i in range(len(arrays))},
        compiler_params=pltpu.CompilerParams(vmem_limit_bytes=2 * MIB),
        cost_estimate=cost(microseconds),
        name="gate",
    )(*arrays, *after)


def origin(place_ref, pair, chips):
    return lax.rem(place_ref[1] + (chips - pair), chips)


def owns(place_ref, pair, chips):
    return (lax.div(origin(place_ref, pair, chips), chips // 2) == place_ref[0]).astype(jnp.int32)


def spot(place_ref, pair, chips):
    return lax.rem(origin(place_ref, pair, chips), chips // 2)


def pick_kernel(place_ref, near_ref, *refs, pair, chips, count):
    far_refs, out_ref = refs[:count], refs[-1]
    keep = owns(place_ref, pair, chips) == 1
    rows = near_ref.shape[0] // len(far_refs)
    for index, far_ref in enumerate(far_refs):
        part = slice(index * rows, (index + 1) * rows)
        out_ref[part, :] = jnp.where(keep, far_ref[...], near_ref[part, :])


def pick_other(place, near, far, pair, chips, after):
    rows, width = near.shape
    whole = pl.BlockSpec(memory_space=pltpu.VMEM)
    return pl.pallas_call(
        functools.partial(pick_kernel, pair=pair, chips=chips, count=len(far)),
        in_specs=[pl.BlockSpec(memory_space=pltpu.SMEM)]
        + [whole] * (1 + len(far))
        + [pl.BlockSpec(memory_space=pl.ANY)] * len(after),
        out_specs=whole,
        out_shape=pltpu.VMEM((rows, width), near.dtype),
        compiler_params=pltpu.CompilerParams(vmem_limit_bytes=4 * MIB),
        cost_estimate=cost(0.01),
        name="pick_other",
    )(place, near, *far, *after)


def fork_kernel(place_ref, down_ref, up_ref, old_down_ref, old_up_ref, *out_refs, chips):
    first_ref, third_ref, top_ref, bottom_ref = out_refs
    half = top_ref.shape[0]
    top_ref[...] = down_ref[:half, :]
    bottom_ref[...] = up_ref[half:, :]
    first_ref[...] = jnp.where(
        owns(place_ref, 1, chips) == 1, up_ref[...], old_down_ref[...]
    )
    third_ref[...] = jnp.where(
        owns(place_ref, 3, chips) == 1, old_up_ref[...], down_ref[...]
    )


def fork(place, down, up, old_down, old_up, chips):
    rows, width = down.shape
    vmem = pl.BlockSpec(memory_space=pltpu.VMEM)
    return pl.pallas_call(
        functools.partial(fork_kernel, chips=chips),
        in_specs=[pl.BlockSpec(memory_space=pltpu.SMEM)] + [vmem] * 4,
        out_specs=[vmem] * 4,
        out_shape=[jax.ShapeDtypeStruct((rows, width), down.dtype)] * 2
        + [jax.ShapeDtypeStruct((rows // 2, width), down.dtype)] * 2,
        compiler_params=pltpu.CompilerParams(vmem_limit_bytes=6 * MIB),
        cost_estimate=cost(0.01),
        name="fork",
    )(place, down, up, old_down, old_up)


def weight_kernel(place_ref, *refs, pairs, pieces, chips, dp_count, known, keep_att):
    count = len(pairs)
    near, refs = refs[:count], refs[count:]
    recv, refs = refs[:count], refs[count:]
    far, refs = refs[: count * pieces], refs[count * pieces :]
    att_refs, carried_ref, refs = refs[:2], refs[2], refs[3:]
    known_refs, refs = refs[:known], refs[known:]
    out_ref, peak_ref, *kept_refs, atts, mine, other, carried, terms, sems, out_sems = refs
    rows, width = att_refs[0].shape
    block = carried.shape[1]
    share = block // dp_count
    part_rows = rows // pieces
    groups = width // LANES
    peak_rows = 8 * groups

    def part(piece):
        return slice(piece * part_rows, (piece + 1) * part_rows)

    def fetch_mine(index, piece, from_near):
        source = near[index].at[part(piece)] if from_near else far[index * pieces + piece]
        return pltpu.make_async_copy(source, mine.at[index, part(piece)], sems.at[1 + piece, index])

    def fetch_other(index):
        return pltpu.make_async_copy(recv[index], other.at[index], sems.at[0, index])

    def fetch_att(side):
        return pltpu.make_async_copy(att_refs[side], atts.at[side], sems.at[3, side])

    def fetch_carried(index):
        place = 2 * spot(place_ref, pairs[index // 2], chips) + index % 2
        return pltpu.make_async_copy(carried_ref.at[place], carried.at[index], sems.at[4, index])

    def send(index):
        if known:
            place = pl.ds(index * groups * share, groups * share if index < 2 * count else peak_rows)
            return pltpu.make_async_copy(
                terms.at[:, place], out_ref.at[:, place], out_sems.at[index]
            )
        place = pl.ds(index * share, share)
        return pltpu.make_async_copy(terms.at[index], out_ref.at[:, place], out_sems.at[index])

    def keep_copy():
        return pltpu.make_async_copy(atts.at[1], kept_refs[0], out_sems.at[2 * count])

    fetch_att(0).start()
    for index, pair in enumerate(pairs):
        keep = owns(place_ref, pair, chips) == 1
        for piece in range(pieces):
            pl.when(keep)(fetch_mine(index, piece, True).start)
            pl.when(jnp.logical_not(keep))(fetch_mine(index, piece, False).start)
        fetch_other(index).start()
        if index == 0:
            fetch_att(1).start()
        fetch_carried(2 * index).start()
        fetch_carried(2 * index + 1).start()
    fetch_att(0).wait()
    for index in range(count):
        for piece in range(pieces):
            fetch_mine(index, piece, True).wait()
        for half in range(2):
            columns = slice(half * block, (half + 1) * block)
            corrected = dot_on(mine[index, :, columns], atts[0], 0, 0)
            if half == 0:
                fetch_other(index).wait()
                if index == 0:
                    fetch_att(1).wait()
                    if keep_att:
                        keep_copy().start()
            corrected = corrected + dot_on(other[index, :, columns], atts[1], 0, 0)
            slot = 2 * index + half
            fetch_carried(slot).wait()
            corrected = corrected + carried[slot]
            peak_ref[slot : slot + 1, :] = jnp.max(jnp.abs(corrected), axis=0, keepdims=True)
            rounded = corrected.astype(BF16).reshape(dp_count, share, width)
            if known:
                for group in range(groups):
                    row = (slot * groups + group) * share
                    lanes = slice(group * LANES, (group + 1) * LANES)
                    terms[:, row : row + share, :] = rounded[:, :, lanes]
            else:
                terms[slot] = rounded
            send(slot).start()
    slots = 2 * count
    if known:
        peaks = jnp.concatenate([peak_ref[...]] + [ref[...] for ref in known_refs], 0)
        peaks = jnp.concatenate(
            [peaks[:, group * LANES : (group + 1) * LANES] for group in range(groups)], 0
        ).astype(BF16)
        for dest in range(dp_count):
            terms[dest, slots * groups * share :, :] = peaks
        send(slots).start()
        slots += 1
    for slot in range(slots):
        send(slot).wait()
    if keep_att:
        keep_copy().wait()


def weight_block(place, near, far, recv, att, carried, known, pairs, chips, dp_count, keep_att):
    rows, width = att[0].shape
    block = carried.shape[1]
    share = block // dp_count
    count = len(pairs)
    pieces = len(far[0])
    if known:
        groups = width // LANES
        out_rows = 2 * count * groups * share + 8 * groups
        out_shape = pltpu.HBM((dp_count, out_rows, LANES), BF16)
        terms = pltpu.VMEM((dp_count, out_rows, LANES), BF16)
    else:
        out_shape = pltpu.HBM((dp_count, 2 * count * share, width), BF16)
        terms = pltpu.VMEM((2 * count, dp_count, share, width), BF16)
    vmem = pl.BlockSpec(memory_space=pltpu.VMEM)
    anywhere = pl.BlockSpec(memory_space=pl.ANY)
    hbm = pl.BlockSpec(memory_space=pltpu.HBM)
    return pl.pallas_call(
        functools.partial(
            weight_kernel,
            pairs=pairs,
            pieces=pieces,
            chips=chips,
            dp_count=dp_count,
            known=len(known),
            keep_att=keep_att,
        ),
        in_specs=[pl.BlockSpec(memory_space=pltpu.SMEM)]
        + [anywhere] * (count * (2 + pieces) + 2)
        + [hbm]
        + [vmem] * len(known),
        out_specs=[hbm, vmem] + [hbm] * keep_att,
        out_shape=[out_shape, jax.ShapeDtypeStruct((2 * count, width), F32)]
        + [pltpu.HBM((rows, width), BF16)] * keep_att,
        scratch_shapes=[
            pltpu.VMEM((2, rows, width), BF16),
            pltpu.VMEM((count, rows, 2 * block), BF16),
            pltpu.VMEM((count, rows, 2 * block), BF16),
            pltpu.VMEM((2 * count, block, width), F32),
            terms,
            pltpu.SemaphoreType.DMA((5, 2 * max(count, 1))),
            pltpu.SemaphoreType.DMA((2 * count + 1,)),
        ],
        compiler_params=pltpu.CompilerParams(vmem_limit_bytes=20 * MIB),
        cost_estimate=cost(0.1),
        name="weight_block",
    )(place, *near, *recv, *[p for f in far for p in f], *att, carried, *known)


def add_kernel(a_ref, b_ref, c_ref, d_ref, first_ref, second_ref):
    first_ref[...] = (a_ref[...].astype(F32) + b_ref[...].astype(F32)).astype(BF16)
    second_ref[...] = (c_ref[...].astype(F32) + d_ref[...].astype(F32)).astype(BF16)


def add_pairs(a, b, c, d):
    rows, width = a.shape
    spec = pl.BlockSpec((rows // 4, width), lambda i: (i, 0))
    return pl.pallas_call(
        add_kernel,
        grid=(4,),
        in_specs=[spec] * 4,
        out_specs=[spec] * 2,
        out_shape=[jax.ShapeDtypeStruct((rows, width), BF16)] * 2,
        compiler_params=pltpu.CompilerParams(vmem_limit_bytes=8 * MIB),
        cost_estimate=cost(0.1),
        name="add_pairs",
    )(a, b, c, d)


def finish_kernel(place_ref, last_ref, sides_ref, middle_ref, levels_ref, scale_ref, *, chips):
    share, width = levels_ref.shape[1:]
    groups = width // LANES
    rows = 2 * groups * share
    total = jnp.sum(last_ref[:, :rows, :].astype(F32), axis=0)
    peaks = jnp.max(last_ref[:, rows:, :].astype(F32), axis=0)
    scale = jnp.concatenate([peaks[group * 8 : group * 8 + 8] for group in range(groups)], 1)
    scale = (scale + 1e-6) / 7.0
    for index, pair in enumerate((0, 1, 3, 2)):
        for half in range(2):
            block = 2 * spot(place_ref, pair, chips) + half
            row = scale[2 * index + half : 2 * index + half + 1]
            scale_ref[pl.ds(block, 1), :] = row
            if pair == 0:
                pieces = [
                    total[(half * groups + group) * share : (half * groups + group + 1) * share]
                    for group in range(groups)
                ]
                terms = jnp.concatenate(pieces, 1)
            else:
                terms_ref = middle_ref if pair == 2 else sides_ref
                start = ((pair == 3) * 2 + half) * share
                terms = terms_ref[pl.ds(start, share), :]
            levels_ref[block] = terms / row


def finish(place, last, sides, middle, share, chips):
    width = middle.shape[1]
    vmem = pl.BlockSpec(memory_space=pltpu.VMEM)
    return pl.pallas_call(
        functools.partial(finish_kernel, chips=chips),
        in_specs=[pl.BlockSpec(memory_space=pltpu.SMEM)] + [vmem] * 3,
        out_specs=[vmem] * 2,
        out_shape=[
            jax.ShapeDtypeStruct((8, share, width), F32),
            jax.ShapeDtypeStruct((8, width), F32),
        ],
        compiler_params=pltpu.CompilerParams(vmem_limit_bytes=12 * MIB),
        cost_estimate=cost(0.1),
        name="finish",
    )(place, last, sides, middle)


def body(query_in, key_in, value_in, attn_grad, out_grad, carried_error, lengths):
    dp_count = lax.axis_size("dp")
    z_count = lax.axis_size("tensor")
    seq = lax.axis_index("seq")
    z = lax.axis_index("tensor")
    up = [(i, (i + 1) % z_count) for i in range(z_count)]
    down = [(i, (i - 1) % z_count) for i in range(z_count)]
    swap = [(0, 1), (1, 0)]

    def peer(array):
        return lax.ppermute(array, "seq", swap)

    own = out_grad[0]
    place = jnp.concatenate([jnp.stack([seq, z]).astype(jnp.int32), lengths[0]])
    heads = own.shape[1] // HEAD_DIM

    def send_up(array):
        return lax.ppermute(array, "tensor", up)

    def send_down(array):
        return lax.ppermute(array, "tensor", down)

    def stay(array):
        return pltpu.with_memory_space_constraint(array, pltpu.HBM)

    from_down, from_up = {1: send_up(own)}, {1: send_down(own)}
    tokens = (
        stay(query_in[0]),
        stay(key_in[0]),
        peer(key_in[0]),
        stay(value_in[0]),
        peer(value_in[0]),
        stay(attn_grad[0]),
    )
    carried = stay(carried_error[0])
    *held, token = attention(place, *tokens, 0, heads // 2, [], [])
    (from_down[1],) = gate([from_down[1]], [token])
    from_down[2] = send_up(from_down[1])
    (from_up[1],) = gate([from_up[1]], [token])
    from_up[2] = send_down(from_up[1])
    att, dq, dk_own, dk_peer, dv_own, dv_peer, token = attention(
        place, *tokens, heads // 2, heads // 2, held, [from_down[1], from_up[1]]
    )
    from_down[2], att = gate([from_down[2], att], [token])
    from_down[3] = send_up(from_down[2])
    (from_up[2],) = gate([from_up[2]], [token])
    from_up[3] = send_down(from_up[2])
    share = carried.shape[1] // dp_count

    def swapped(pair, near, far, after=()):
        return peer(pick_other(place, near, far, pair, z_count, after))

    def weigh(pairs, near, far, recv, atts, known=(), keep_att=False):
        return weight_block(
            place, near, far, recv, atts, carried, known, pairs, z_count, dp_count, keep_att
        )

    def exchange(array):
        return lax.all_to_all(array, "dp", 0, 0, tiled=True)

    recv2 = swapped(2, from_down[2], [from_up[2]])
    terms, peaks2, att_peer = weigh(
        (2,), [from_down[2]], [[from_up[2]]], [recv2], (att, peer(att)), keep_att=True
    )
    atts = (att, stay(att_peer))
    (middle,) = gate([exchange(terms)], [], 1.0)
    from_down[3], from_up[3] = gate([from_down[3], from_up[3]], [peaks2])
    send1, send3, top, bottom = fork(
        place, from_down[3], from_up[3], from_down[1], from_up[1], z_count
    )
    recv13 = [peer(send1), peer(send3)]
    farthest = [send_up(top), send_down(bottom)]
    terms, peaks13 = weigh(
        (1, 3),
        [from_down[1], from_down[3]],
        [[from_up[3]], [from_up[1]]],
        recv13,
        atts,
    )
    farthest = gate(farthest, [peaks13, middle])
    (terms,) = gate([terms], farthest, space=pltpu.HBM)
    (sides,) = gate([exchange(terms)], [])
    recv0 = swapped(0, own, farthest)
    terms, _ = weigh((0,), [own], [farthest], [recv0], atts, (peaks13, peaks2))
    last = exchange(terms)
    d_keys, d_values = add_pairs(dk_own, peer(dk_peer), dv_own, peer(dv_peer))
    level_sums, block_scale = finish(
        place,
        last,
        jnp.sum(sides.astype(F32), axis=0),
        jnp.sum(middle.astype(F32), axis=0),
        share,
        z_count,
    )
    return dq[None], d_keys[None], d_values[None], level_sums, block_scale


def solution(mesh):
    tokens = P("dp", "seq", "tensor")
    in_specs = (tokens,) * 5 + (P("dp", "seq", None, "tensor"), P("dp", None))
    out_specs = (tokens,) * 3 + (P("seq", "dp", "tensor"), P("seq", "tensor"))
    return jax.shard_map(body, mesh=mesh, in_specs=in_specs, out_specs=out_specs, check_vma=False)
```

```python
import functools
import math

import jax
import jax.numpy as jnp
from jax import lax
from jax.experimental import pallas as pl
from jax.experimental.pallas import tpu as pltpu
from jax.sharding import PartitionSpec as P

HEAD_DIM = 128
NEG_FILL = -1e30
F32 = jnp.float32
BF16 = jnp.bfloat16
MIB = 2**20
LANES = 128
TOKEN = jax.ShapeDtypeStruct((8, 128), F32)
TOKEN_SPEC = pl.BlockSpec((8, 128), lambda i, *_: (0, 0))


def dot_on(a, b, a_dim, b_dim):
    return lax.dot_general(a, b, (((a_dim,), (b_dim,)), ((), ())), preferred_element_type=F32)


def attention_kernel(
    place_ref, kp_ref, vp_ref, q_hbm, ko_hbm, vo_hbm, g_hbm, *refs, tile, first, count
):
    att_ref, dq_ref, dko_ref, dkp_ref, dvo_ref, dvp_ref, token_ref = refs[-12:-5]
    ids_ref, dk_acc, dv_acc, held_ref, sems = refs[-5:]
    token_ref[...] = jnp.zeros_like(token_ref)
    rows = kp_ref.shape[0]
    head = pl.program_id(0)

    def fetch(step, source, index):
        column = pl.ds((first + step) * HEAD_DIM, HEAD_DIM)
        return pltpu.make_async_copy(
            source.at[:, column], held_ref.at[step, index], sems.at[step, index]
        )

    sources = (ko_hbm, q_hbm, vo_hbm, g_hbm)

    @pl.when(head == 0)
    def _():
        for step in range(count):
            for index, source in enumerate(sources):
                fetch(step, source, index).start()
    inverse = 1.0 / math.sqrt(HEAD_DIM)
    to_exp2 = inverse * math.log2(math.e)
    own = place_ref[0] * rows
    other = rows - own

    def ids(positions):
        found = jnp.zeros(positions.shape, jnp.int32)
        end = jnp.int32(0)
        for image in range(4):
            end = end + place_ref[2 + image]
            found = found + (positions >= end).astype(jnp.int32)
        return found

    @pl.when(head == 0)
    def _():
        positions = lax.broadcasted_iota(jnp.int32, (rows, 128), 0)
        ids_ref[:rows, :] = ids(positions + own)
        ids_ref[rows:, :] = ids(positions + other)

    for step in range(count):

        @pl.when(head == step)
        def _():
            for index, source in enumerate(sources):
                fetch(step, source, index).wait()

    ko_ref, q_ref, vo_ref, g_ref = (held_ref.at[head, index] for index in range(4))
    k = jnp.concatenate([ko_ref[...], kp_ref[...]], 0)
    v = jnp.concatenate([vo_ref[...], vp_ref[...]], 0)
    k_t, v_t = k.T, v.T
    for i in range(rows // tile):
        part = slice(i * tile, (i + 1) * tile)
        q, g = q_ref[part, :], g_ref[part, :]
        query_ids = ids(lax.broadcasted_iota(jnp.int32, (8, tile), 1) + (own + i * tile))[:1]
        key_ids = jnp.concatenate([ids_ref[...]] * (tile // 128), 1)
        scores = jnp.where(key_ids == query_ids, dot_on(k, q, 1, 1) * to_exp2, NEG_FILL)
        peak = jnp.max(scores, axis=0, keepdims=True)
        raised = jnp.exp2(scores - peak)
        weights = raised * (1.0 / jnp.sum(raised, axis=0, keepdims=True))
        prob = weights.astype(BF16)
        att_t = dot_on(v_t, prob, 1, 0).astype(BF16).astype(F32)
        att_ref[part, :] = att_t.T.astype(BF16)
        delta = jnp.sum(g.astype(F32).T * att_t, axis=0, keepdims=True)
        grad_probs = dot_on(v, g, 1, 1)
        grad_scores = (weights * ((grad_probs - delta) * inverse)).astype(BF16)
        dq_ref[part, :] = dot_on(k_t, grad_scores, 1, 0).T.astype(BF16)
        dk = dot_on(grad_scores, q, 1, 0)
        dv = dot_on(prob, g, 1, 0)
        if i == 0:
            dk_acc[...] = dk
            dv_acc[...] = dv
        else:
            dk_acc[...] += dk
            dv_acc[...] += dv
    dko_ref[...] = dk_acc[:rows].astype(BF16)
    dkp_ref[...] = dk_acc[rows:].astype(BF16)
    dvo_ref[...] = dv_acc[:rows].astype(BF16)
    dvp_ref[...] = dv_acc[rows:].astype(BF16)


def cost(microseconds, *arrays):
    size = sum(array.size * array.dtype.itemsize for array in arrays)
    return pl.CostEstimate(
        flops=int(microseconds * 1.15e9), bytes_accessed=size, transcendentals=0
    )


def attention(place, q, ko, kp, vo, vp, g, first, count, held, after):
    rows, width = q.shape
    spec = pl.BlockSpec((rows, HEAD_DIM), lambda i, *_: (0, i + first))
    return pl.pallas_call(
        functools.partial(attention_kernel, tile=256, first=first, count=count),
        grid_spec=pltpu.PrefetchScalarGridSpec(
            num_scalar_prefetch=1,
            grid=(count,),
            in_specs=[spec] * 2
            + [pl.BlockSpec(memory_space=pltpu.HBM)] * 4
            + [pl.BlockSpec(memory_space=pl.ANY)] * (len(held) + len(after)),
            out_specs=[spec] * 6 + [TOKEN_SPEC],
            scratch_shapes=[
                pltpu.VMEM((2 * rows, 128), jnp.int32),
                pltpu.VMEM((2 * rows, HEAD_DIM), F32),
                pltpu.VMEM((2 * rows, HEAD_DIM), F32),
                pltpu.VMEM((count, 4, rows, HEAD_DIM), BF16),
                pltpu.SemaphoreType.DMA((count, 4)),
            ],
        ),
        out_shape=[pltpu.VMEM((rows, width), BF16)]
        + [pltpu.HBM((rows, width), BF16)] * 5
        + [TOKEN],
        input_output_aliases={7 + i: i for i in range(len(held))},
        compiler_params=pltpu.CompilerParams(vmem_limit_bytes=18 * MIB),
        cost_estimate=cost(0.2),
        name="attention",
    )(place, kp, vp, q, ko, vo, g, *held, *after)


def gate_kernel(*refs):
    pass


def gate(arrays, after, microseconds=0.01, space=jax.ShapeDtypeStruct):
    anywhere = pl.BlockSpec(memory_space=pl.ANY)
    return pl.pallas_call(
        gate_kernel,
        in_specs=[anywhere] * (len(arrays) + len(after)),
        out_specs=[anywhere] * len(arrays),
        out_shape=[space(a.shape, a.dtype) for a in arrays],
        input_output_aliases={i: i for i in range(len(arrays))},
        compiler_params=pltpu.CompilerParams(vmem_limit_bytes=2 * MIB),
        cost_estimate=cost(microseconds),
        name="gate",
    )(*arrays, *after)


def origin(place_ref, pair, chips):
    return lax.rem(place_ref[1] + (chips - pair), chips)


def owns(place_ref, pair, chips):
    return (lax.div(origin(place_ref, pair, chips), chips // 2) == place_ref[0]).astype(jnp.int32)


def spot(place_ref, pair, chips):
    return lax.rem(origin(place_ref, pair, chips), chips // 2)


def pick_kernel(place_ref, near_ref, *refs, pair, chips, count):
    far_refs, out_ref = refs[:count], refs[-1]
    keep = owns(place_ref, pair, chips) == 1
    rows = near_ref.shape[0] // len(far_refs)
    for index, far_ref in enumerate(far_refs):
        part = slice(index * rows, (index + 1) * rows)
        out_ref[part, :] = jnp.where(keep, far_ref[...], near_ref[part, :])


def pick_other(place, near, far, pair, chips, after):
    rows, width = near.shape
    whole = pl.BlockSpec(memory_space=pltpu.VMEM)
    return pl.pallas_call(
        functools.partial(pick_kernel, pair=pair, chips=chips, count=len(far)),
        in_specs=[pl.BlockSpec(memory_space=pltpu.SMEM)]
        + [whole] * (1 + len(far))
        + [pl.BlockSpec(memory_space=pl.ANY)] * len(after),
        out_specs=whole,
        out_shape=pltpu.VMEM((rows, width), near.dtype),
        compiler_params=pltpu.CompilerParams(vmem_limit_bytes=4 * MIB),
        cost_estimate=cost(0.01),
        name="pick_other",
    )(place, near, *far, *after)


def fork_kernel(place_ref, down_ref, up_ref, old_down_ref, old_up_ref, *out_refs, chips):
    first_ref, third_ref, top_ref, bottom_ref = out_refs
    half = top_ref.shape[0]
    top_ref[...] = down_ref[:half, :]
    bottom_ref[...] = up_ref[half:, :]
    first_ref[...] = jnp.where(
        owns(place_ref, 1, chips) == 1, up_ref[...], old_down_ref[...]
    )
    third_ref[...] = jnp.where(
        owns(place_ref, 3, chips) == 1, old_up_ref[...], down_ref[...]
    )


def fork(place, down, up, old_down, old_up, chips):
    rows, width = down.shape
    vmem = pl.BlockSpec(memory_space=pltpu.VMEM)
    return pl.pallas_call(
        functools.partial(fork_kernel, chips=chips),
        in_specs=[pl.BlockSpec(memory_space=pltpu.SMEM)] + [vmem] * 4,
        out_specs=[vmem] * 4,
        out_shape=[jax.ShapeDtypeStruct((rows, width), down.dtype)] * 2
        + [jax.ShapeDtypeStruct((rows // 2, width), down.dtype)] * 2,
        compiler_params=pltpu.CompilerParams(vmem_limit_bytes=6 * MIB),
        cost_estimate=cost(0.01),
        name="fork",
    )(place, down, up, old_down, old_up)


def weight_kernel(
    place_ref, *refs, pairs, pieces, choices, chips, dp_count, known, keep_att
):
    count = len(pairs)
    near, refs = refs[:count], refs[count:]
    recv, refs = refs[: count * choices], refs[count * choices :]
    far, refs = refs[: count * pieces], refs[count * pieces :]
    att_refs, carried_ref, refs = refs[:2], refs[2], refs[3:]
    known_refs, refs = refs[:known], refs[known:]
    out_ref, peak_ref, *kept_refs, atts, mine, other, carried, terms, sems, out_sems = refs
    rows, width = att_refs[0].shape
    block = carried.shape[1]
    share = block // dp_count
    part_rows = rows // pieces
    groups = width // LANES
    peak_rows = 8 * groups

    def part(piece):
        return slice(piece * part_rows, (piece + 1) * part_rows)

    def fetch_mine(index, piece, from_near):
        source = near[index].at[part(piece)] if from_near else far[index * pieces + piece]
        return pltpu.make_async_copy(source, mine.at[index, part(piece)], sems.at[1 + piece, index])

    def fetch_other(index, choice=0):
        return pltpu.make_async_copy(
            recv[index * choices + choice], other.at[index], sems.at[0, index]
        )

    def fetch_att(side):
        return pltpu.make_async_copy(att_refs[side], atts.at[side], sems.at[3, side])

    def fetch_carried(index):
        place = 2 * spot(place_ref, pairs[index // 2], chips) + index % 2
        return pltpu.make_async_copy(carried_ref.at[place], carried.at[index], sems.at[4, index])

    def send(index):
        if known:
            place = pl.ds(index * groups * share, groups * share if index < 2 * count else peak_rows)
            return pltpu.make_async_copy(
                terms.at[:, place], out_ref.at[:, place], out_sems.at[index]
            )
        place = pl.ds(index * share, share)
        return pltpu.make_async_copy(terms.at[index], out_ref.at[:, place], out_sems.at[index])

    def keep_copy():
        return pltpu.make_async_copy(atts.at[1], kept_refs[0], out_sems.at[2 * count])

    fetch_att(0).start()
    for index, pair in enumerate(pairs):
        keep = owns(place_ref, pair, chips) == 1
        for piece in range(pieces):
            pl.when(keep)(fetch_mine(index, piece, True).start)
            pl.when(jnp.logical_not(keep))(fetch_mine(index, piece, False).start)
        if choices == 1:
            fetch_other(index).start()
        else:
            pl.when(keep)(fetch_other(index, 0).start)
            pl.when(jnp.logical_not(keep))(fetch_other(index, 1).start)
        if index == 0:
            fetch_att(1).start()
        fetch_carried(2 * index).start()
        fetch_carried(2 * index + 1).start()
    fetch_att(0).wait()
    for index in range(count):
        for piece in range(pieces):
            fetch_mine(index, piece, True).wait()
        for half in range(2):
            columns = slice(half * block, (half + 1) * block)
            corrected = dot_on(mine[index, :, columns], atts[0], 0, 0)
            if half == 0:
                fetch_other(index).wait()
                if index == 0:
                    fetch_att(1).wait()
                    if keep_att:
                        keep_copy().start()
            corrected = corrected + dot_on(other[index, :, columns], atts[1], 0, 0)
            slot = 2 * index + half
            fetch_carried(slot).wait()
            corrected = corrected + carried[slot]
            peak_ref[slot : slot + 1, :] = jnp.max(jnp.abs(corrected), axis=0, keepdims=True)
            rounded = corrected.astype(BF16).reshape(dp_count, share, width)
            if known:
                for group in range(groups):
                    row = (slot * groups + group) * share
                    lanes = slice(group * LANES, (group + 1) * LANES)
                    terms[:, row : row + share, :] = rounded[:, :, lanes]
            else:
                terms[slot] = rounded
            send(slot).start()
    slots = 2 * count
    if known:
        peaks = jnp.concatenate([peak_ref[...]] + [ref[...] for ref in known_refs], 0)
        peaks = jnp.concatenate(
            [peaks[:, group * LANES : (group + 1) * LANES] for group in range(groups)], 0
        ).astype(BF16)
        for dest in range(dp_count):
            terms[dest, slots * groups * share :, :] = peaks
        send(slots).start()
        slots += 1
    for slot in range(slots):
        send(slot).wait()
    if keep_att:
        keep_copy().wait()


def weight_block(place, near, far, recv, att, carried, known, pairs, chips, dp_count, keep_att):
    rows, width = att[0].shape
    block = carried.shape[1]
    share = block // dp_count
    count = len(pairs)
    pieces = len(far[0])
    if known:
        groups = width // LANES
        out_rows = 2 * count * groups * share + 8 * groups
        out_shape = pltpu.HBM((dp_count, out_rows, LANES), BF16)
        terms = pltpu.VMEM((dp_count, out_rows, LANES), BF16)
    else:
        out_shape = pltpu.HBM((dp_count, 2 * count * share, width), BF16)
        terms = pltpu.VMEM((2 * count, dp_count, share, width), BF16)
    vmem = pl.BlockSpec(memory_space=pltpu.VMEM)
    anywhere = pl.BlockSpec(memory_space=pl.ANY)
    hbm = pl.BlockSpec(memory_space=pltpu.HBM)
    return pl.pallas_call(
        functools.partial(
            weight_kernel,
            pairs=pairs,
            pieces=pieces,
            choices=len(recv) // count,
            chips=chips,
            dp_count=dp_count,
            known=len(known),
            keep_att=keep_att,
        ),
        in_specs=[pl.BlockSpec(memory_space=pltpu.SMEM)]
        + [anywhere] * (count * (1 + pieces) + len(recv) + 2)
        + [hbm]
        + [vmem] * len(known),
        out_specs=[hbm, vmem] + [hbm] * keep_att,
        out_shape=[out_shape, jax.ShapeDtypeStruct((2 * count, width), F32)]
        + [pltpu.HBM((rows, width), BF16)] * keep_att,
        scratch_shapes=[
            pltpu.VMEM((2, rows, width), BF16),
            pltpu.VMEM((count, rows, 2 * block), BF16),
            pltpu.VMEM((count, rows, 2 * block), BF16),
            pltpu.VMEM((2 * count, block, width), F32),
            terms,
            pltpu.SemaphoreType.DMA((5, 2 * max(count, 1))),
            pltpu.SemaphoreType.DMA((2 * count + 1,)),
        ],
        compiler_params=pltpu.CompilerParams(vmem_limit_bytes=20 * MIB),
        cost_estimate=cost(0.1),
        name="weight_block",
    )(place, *near, *recv, *[p for f in far for p in f], *att, carried, *known)


def add_kernel(a_ref, b_ref, c_ref, d_ref, first_ref, second_ref):
    first_ref[...] = (a_ref[...].astype(F32) + b_ref[...].astype(F32)).astype(BF16)
    second_ref[...] = (c_ref[...].astype(F32) + d_ref[...].astype(F32)).astype(BF16)


def add_pairs(a, b, c, d):
    rows, width = a.shape
    spec = pl.BlockSpec((rows // 4, width), lambda i: (i, 0))
    return pl.pallas_call(
        add_kernel,
        grid=(4,),
        in_specs=[spec] * 4,
        out_specs=[spec] * 2,
        out_shape=[jax.ShapeDtypeStruct((rows, width), BF16)] * 2,
        compiler_params=pltpu.CompilerParams(vmem_limit_bytes=8 * MIB),
        cost_estimate=cost(0.1),
        name="add_pairs",
    )(a, b, c, d)


def finish_kernel(place_ref, last_ref, sides_ref, middle_ref, levels_ref, scale_ref, *, chips):
    share, width = levels_ref.shape[1:]
    groups = width // LANES
    rows = 2 * groups * share
    total = jnp.sum(last_ref[:, :rows, :].astype(F32), axis=0)
    peaks = jnp.max(last_ref[:, rows:, :].astype(F32), axis=0)
    scale = jnp.concatenate([peaks[group * 8 : group * 8 + 8] for group in range(groups)], 1)
    scale = (scale + 1e-6) / 7.0
    for index, pair in enumerate((0, 1, 3, 2)):
        for half in range(2):
            block = 2 * spot(place_ref, pair, chips) + half
            row = scale[2 * index + half : 2 * index + half + 1]
            scale_ref[pl.ds(block, 1), :] = row
            if pair == 0:
                pieces = [
                    total[(half * groups + group) * share : (half * groups + group + 1) * share]
                    for group in range(groups)
                ]
                terms = jnp.concatenate(pieces, 1)
            else:
                terms_ref = middle_ref if pair == 2 else sides_ref
                start = ((pair == 3) * 2 + half) * share
                terms = terms_ref[pl.ds(start, share), :]
            levels_ref[block] = terms / row


def finish(place, last, sides, middle, share, chips):
    width = middle.shape[1]
    vmem = pl.BlockSpec(memory_space=pltpu.VMEM)
    return pl.pallas_call(
        functools.partial(finish_kernel, chips=chips),
        in_specs=[pl.BlockSpec(memory_space=pltpu.SMEM)] + [vmem] * 3,
        out_specs=[vmem] * 2,
        out_shape=[
            jax.ShapeDtypeStruct((8, share, width), F32),
            jax.ShapeDtypeStruct((8, width), F32),
        ],
        compiler_params=pltpu.CompilerParams(vmem_limit_bytes=12 * MIB),
        cost_estimate=cost(0.1),
        name="finish",
    )(place, last, sides, middle)


def body(query_in, key_in, value_in, attn_grad, out_grad, carried_error, lengths):
    dp_count = lax.axis_size("dp")
    z_count = lax.axis_size("tensor")
    seq = lax.axis_index("seq")
    z = lax.axis_index("tensor")
    up = [(i, (i + 1) % z_count) for i in range(z_count)]
    down = [(i, (i - 1) % z_count) for i in range(z_count)]
    swap = [(0, 1), (1, 0)]

    def peer(array):
        return lax.ppermute(array, "seq", swap)

    own = out_grad[0]
    place = jnp.concatenate([jnp.stack([seq, z]).astype(jnp.int32), lengths[0]])
    heads = own.shape[1] // HEAD_DIM

    def send_up(array):
        return lax.ppermute(array, "tensor", up)

    def send_down(array):
        return lax.ppermute(array, "tensor", down)

    def stay(array):
        return pltpu.with_memory_space_constraint(array, pltpu.HBM)

    from_down, from_up = {1: send_up(own)}, {1: send_down(own)}
    tokens = (
        stay(query_in[0]),
        stay(key_in[0]),
        peer(key_in[0]),
        stay(value_in[0]),
        peer(value_in[0]),
        stay(attn_grad[0]),
    )
    carried = stay(carried_error[0])
    *held, token = attention(place, *tokens, 0, heads // 2, [], [])
    (from_down[1],) = gate([from_down[1]], [token])
    from_down[2] = send_up(from_down[1])
    (from_up[1],) = gate([from_up[1]], [token])
    from_up[2] = send_down(from_up[1])
    att, dq, dk_own, dk_peer, dv_own, dv_peer, token = attention(
        place, *tokens, heads // 2, heads // 2, held, [from_down[1], from_up[1]]
    )
    from_down[2], att = gate([from_down[2], att], [token])
    from_down[3] = send_up(from_down[2])
    (from_up[2],) = gate([from_up[2]], [token])
    from_up[3] = send_down(from_up[2])
    share = carried.shape[1] // dp_count

    def swapped(pair, near, far, after=()):
        return peer(pick_other(place, near, far, pair, z_count, after))

    def weigh(pairs, near, far, recv, atts, known=(), keep_att=False):
        return weight_block(
            place, near, far, recv, atts, carried, known, pairs, z_count, dp_count, keep_att
        )

    def exchange(array):
        return lax.all_to_all(array, "dp", 0, 0, tiled=True)

    recv2 = [peer(from_down[2]), peer(from_up[2])]
    terms, peaks2, att_peer = weigh(
        (2,), [from_down[2]], [[from_up[2]]], recv2, (att, peer(att)), keep_att=True
    )
    atts = (att, stay(att_peer))
    (middle,) = gate([exchange(terms)], [], 1.0)
    from_down[3], from_up[3] = gate([from_down[3], from_up[3]], [peaks2])
    send1, send3, top, bottom = fork(
        place, from_down[3], from_up[3], from_down[1], from_up[1], z_count
    )
    recv13 = [peer(send1), peer(send3)]
    farthest = [send_up(top), send_down(bottom)]
    terms, peaks13 = weigh(
        (1, 3),
        [from_down[1], from_down[3]],
        [[from_up[3]], [from_up[1]]],
        recv13,
        atts,
    )
    farthest = gate(farthest, [peaks13, middle])
    (terms,) = gate([terms], farthest, space=pltpu.HBM)
    (sides,) = gate([exchange(terms)], [])
    recv0 = swapped(0, own, farthest)
    terms, _ = weigh((0,), [own], [farthest], [recv0], atts, (peaks13, peaks2))
    last = exchange(terms)
    d_keys, d_values = add_pairs(dk_own, peer(dk_peer), dv_own, peer(dv_peer))
    level_sums, block_scale = finish(
        place,
        last,
        jnp.sum(sides.astype(F32), axis=0),
        jnp.sum(middle.astype(F32), axis=0),
        share,
        z_count,
    )
    return dq[None], d_keys[None], d_values[None], level_sums, block_scale


def solution(mesh):
    tokens = P("dp", "seq", "tensor")
    in_specs = (tokens,) * 5 + (P("dp", "seq", None, "tensor"), P("dp", None))
    out_specs = (tokens,) * 3 + (P("seq", "dp", "tensor"), P("seq", "tensor"))
    return jax.shard_map(body, mesh=mesh, in_specs=in_specs, out_specs=out_specs, check_vma=False)
```

```python
import functools
import math

import jax
import jax.numpy as jnp
from jax import lax
from jax.experimental import pallas as pl
from jax.experimental.pallas import tpu as pltpu
from jax.sharding import PartitionSpec as P

HEAD_DIM = 128
NEG_FILL = -1e30
F32 = jnp.float32
BF16 = jnp.bfloat16
MIB = 2**20
LANES = 128
TOKEN = jax.ShapeDtypeStruct((8, 128), F32)
TOKEN_SPEC = pl.BlockSpec((8, 128), lambda i, *_: (0, 0))


def dot_on(a, b, a_dim, b_dim):
    return lax.dot_general(a, b, (((a_dim,), (b_dim,)), ((), ())), preferred_element_type=F32)


def attention_kernel(
    place_ref, kp_ref, vp_ref, q_hbm, ko_hbm, vo_hbm, g_hbm, *refs, tile, first, count
):
    att_ref, dq_ref, dko_ref, dkp_ref, dvo_ref, dvp_ref, token_ref = refs[-12:-5]
    ids_ref, dk_acc, dv_acc, held_ref, sems = refs[-5:]
    token_ref[...] = jnp.zeros_like(token_ref)
    rows = kp_ref.shape[0]
    head = pl.program_id(0)

    def fetch(step, source, index):
        column = pl.ds((first + step) * HEAD_DIM, HEAD_DIM)
        return pltpu.make_async_copy(
            source.at[:, column], held_ref.at[step, index], sems.at[step, index]
        )

    sources = (ko_hbm, q_hbm, vo_hbm, g_hbm)

    @pl.when(head == 0)
    def _():
        for step in range(count):
            for index, source in enumerate(sources):
                fetch(step, source, index).start()
    inverse = 1.0 / math.sqrt(HEAD_DIM)
    to_exp2 = inverse * math.log2(math.e)
    own = place_ref[0] * rows
    other = rows - own

    def ids(positions):
        found = jnp.zeros(positions.shape, jnp.int32)
        end = jnp.int32(0)
        for image in range(4):
            end = end + place_ref[2 + image]
            found = found + (positions >= end).astype(jnp.int32)
        return found

    @pl.when(head == 0)
    def _():
        positions = lax.broadcasted_iota(jnp.int32, (rows, 128), 0)
        ids_ref[:rows, :] = ids(positions + own)
        ids_ref[rows:, :] = ids(positions + other)

    for step in range(count):

        @pl.when(head == step)
        def _():
            for index, source in enumerate(sources):
                fetch(step, source, index).wait()

    ko_ref, q_ref, vo_ref, g_ref = (held_ref.at[head, index] for index in range(4))
    k = jnp.concatenate([ko_ref[...], kp_ref[...]], 0)
    v = jnp.concatenate([vo_ref[...], vp_ref[...]], 0)
    k_t, v_t = k.T, v.T
    for i in range(rows // tile):
        part = slice(i * tile, (i + 1) * tile)
        q, g = q_ref[part, :], g_ref[part, :]
        query_ids = ids(lax.broadcasted_iota(jnp.int32, (8, tile), 1) + (own + i * tile))[:1]
        key_ids = jnp.concatenate([ids_ref[...]] * (tile // 128), 1)
        scores = jnp.where(key_ids == query_ids, dot_on(k, q, 1, 1) * to_exp2, NEG_FILL)
        peak = jnp.max(scores, axis=0, keepdims=True)
        raised = jnp.exp2(scores - peak)
        weights = raised * (1.0 / jnp.sum(raised, axis=0, keepdims=True))
        prob = weights.astype(BF16)
        att_t = dot_on(v_t, prob, 1, 0).astype(BF16).astype(F32)
        att_ref[part, :] = att_t.T.astype(BF16)
        delta = jnp.sum(g.astype(F32).T * att_t, axis=0, keepdims=True)
        grad_probs = dot_on(v, g, 1, 1)
        grad_scores = (weights * ((grad_probs - delta) * inverse)).astype(BF16)
        dq_ref[part, :] = dot_on(k_t, grad_scores, 1, 0).T.astype(BF16)
        dk = dot_on(grad_scores, q, 1, 0)
        dv = dot_on(prob, g, 1, 0)
        if i == 0:
            dk_acc[...] = dk
            dv_acc[...] = dv
        else:
            dk_acc[...] += dk
            dv_acc[...] += dv
    dko_ref[...] = dk_acc[:rows].astype(BF16)
    dkp_ref[...] = dk_acc[rows:].astype(BF16)
    dvo_ref[...] = dv_acc[:rows].astype(BF16)
    dvp_ref[...] = dv_acc[rows:].astype(BF16)


def cost(microseconds, *arrays):
    size = sum(array.size * array.dtype.itemsize for array in arrays)
    return pl.CostEstimate(
        flops=int(microseconds * 1.15e9), bytes_accessed=size, transcendentals=0
    )


def attention(place, q, ko, kp, vo, vp, g, first, count, held, after):
    rows, width = q.shape
    spec = pl.BlockSpec((rows, HEAD_DIM), lambda i, *_: (0, i + first))
    return pl.pallas_call(
        functools.partial(attention_kernel, tile=256, first=first, count=count),
        grid_spec=pltpu.PrefetchScalarGridSpec(
            num_scalar_prefetch=1,
            grid=(count,),
            in_specs=[spec] * 2
            + [pl.BlockSpec(memory_space=pltpu.HBM)] * 4
            + [pl.BlockSpec(memory_space=pl.ANY)] * (len(held) + len(after)),
            out_specs=[spec] * 6 + [TOKEN_SPEC],
            scratch_shapes=[
                pltpu.VMEM((2 * rows, 128), jnp.int32),
                pltpu.VMEM((2 * rows, HEAD_DIM), F32),
                pltpu.VMEM((2 * rows, HEAD_DIM), F32),
                pltpu.VMEM((count, 4, rows, HEAD_DIM), BF16),
                pltpu.SemaphoreType.DMA((count, 4)),
            ],
        ),
        out_shape=[pltpu.VMEM((rows, width), BF16)]
        + [pltpu.HBM((rows, width), BF16)] * 5
        + [TOKEN],
        input_output_aliases={7 + i: i for i in range(len(held))},
        compiler_params=pltpu.CompilerParams(vmem_limit_bytes=18 * MIB),
        cost_estimate=cost(0.2),
        name="attention",
    )(place, kp, vp, q, ko, vo, g, *held, *after)


def gate_kernel(*refs):
    pass


def gate(arrays, after, microseconds=0.01, space=jax.ShapeDtypeStruct):
    anywhere = pl.BlockSpec(memory_space=pl.ANY)
    return pl.pallas_call(
        gate_kernel,
        in_specs=[anywhere] * (len(arrays) + len(after)),
        out_specs=[anywhere] * len(arrays),
        out_shape=[space(a.shape, a.dtype) for a in arrays],
        input_output_aliases={i: i for i in range(len(arrays))},
        compiler_params=pltpu.CompilerParams(vmem_limit_bytes=2 * MIB),
        cost_estimate=cost(microseconds),
        name="gate",
    )(*arrays, *after)


def origin(place_ref, pair, chips):
    return lax.rem(place_ref[1] + (chips - pair), chips)


def owns(place_ref, pair, chips):
    return (lax.div(origin(place_ref, pair, chips), chips // 2) == place_ref[0]).astype(jnp.int32)


def spot(place_ref, pair, chips):
    return lax.rem(origin(place_ref, pair, chips), chips // 2)


def pick_kernel(place_ref, near_ref, *refs, pair, chips, count):
    far_refs, out_ref = refs[:count], refs[-1]
    keep = owns(place_ref, pair, chips) == 1
    rows = near_ref.shape[0] // len(far_refs)
    for index, far_ref in enumerate(far_refs):
        part = slice(index * rows, (index + 1) * rows)
        out_ref[part, :] = jnp.where(keep, far_ref[...], near_ref[part, :])


def pick_other(place, near, far, pair, chips, after):
    rows, width = near.shape
    whole = pl.BlockSpec(memory_space=pltpu.VMEM)
    return pl.pallas_call(
        functools.partial(pick_kernel, pair=pair, chips=chips, count=len(far)),
        in_specs=[pl.BlockSpec(memory_space=pltpu.SMEM)]
        + [whole] * (1 + len(far))
        + [pl.BlockSpec(memory_space=pl.ANY)] * len(after),
        out_specs=whole,
        out_shape=pltpu.VMEM((rows, width), near.dtype),
        compiler_params=pltpu.CompilerParams(vmem_limit_bytes=4 * MIB),
        cost_estimate=cost(0.01),
        name="pick_other",
    )(place, near, *far, *after)


def fork_kernel(place_ref, down_ref, up_ref, old_down_ref, old_up_ref, *out_refs, chips):
    first_ref, third_ref, top_ref, bottom_ref = out_refs
    half = top_ref.shape[0]
    top_ref[...] = down_ref[:half, :]
    bottom_ref[...] = up_ref[half:, :]
    first_ref[...] = jnp.where(
        owns(place_ref, 1, chips) == 1, up_ref[...], old_down_ref[...]
    )
    third_ref[...] = jnp.where(
        owns(place_ref, 3, chips) == 1, old_up_ref[...], down_ref[...]
    )


def fork(place, down, up, old_down, old_up, chips):
    rows, width = down.shape
    vmem = pl.BlockSpec(memory_space=pltpu.VMEM)
    return pl.pallas_call(
        functools.partial(fork_kernel, chips=chips),
        in_specs=[pl.BlockSpec(memory_space=pltpu.SMEM)] + [vmem] * 4,
        out_specs=[vmem] * 4,
        out_shape=[jax.ShapeDtypeStruct((rows, width), down.dtype)] * 2
        + [jax.ShapeDtypeStruct((rows // 2, width), down.dtype)] * 2,
        compiler_params=pltpu.CompilerParams(vmem_limit_bytes=6 * MIB),
        cost_estimate=cost(0.01),
        name="fork",
    )(place, down, up, old_down, old_up)


def weight_kernel(
    place_ref, *refs, pairs, pieces, choices, chips, dp_count, known, keep_att
):
    count = len(pairs)
    near, refs = refs[:count], refs[count:]
    recv, refs = refs[: count * choices], refs[count * choices :]
    far, refs = refs[: count * pieces], refs[count * pieces :]
    att_refs, carried_ref, refs = refs[:2], refs[2], refs[3:]
    known_refs, refs = refs[:known], refs[known:]
    out_ref, peak_ref, *kept_refs, atts, mine, other, carried, terms, sems, out_sems = refs
    rows, width = att_refs[0].shape
    block = carried.shape[1]
    share = block // dp_count
    part_rows = rows // pieces
    groups = width // LANES
    peak_rows = 8 * groups

    def part(piece):
        return slice(piece * part_rows, (piece + 1) * part_rows)

    def fetch_mine(index, piece, from_near):
        source = near[index].at[part(piece)] if from_near else far[index * pieces + piece]
        return pltpu.make_async_copy(source, mine.at[index, part(piece)], sems.at[1 + piece, index])

    def fetch_other(index, choice=0):
        return pltpu.make_async_copy(
            recv[index * choices + choice], other.at[index], sems.at[0, index]
        )

    def fetch_att(side):
        return pltpu.make_async_copy(att_refs[side], atts.at[side], sems.at[3, side])

    def fetch_carried(index):
        place = 2 * spot(place_ref, pairs[index // 2], chips) + index % 2
        return pltpu.make_async_copy(carried_ref.at[place], carried.at[index], sems.at[4, index])

    def send(index):
        if known:
            place = pl.ds(index * groups * share, groups * share if index < 2 * count else peak_rows)
            return pltpu.make_async_copy(
                terms.at[:, place], out_ref.at[:, place], out_sems.at[index]
            )
        place = pl.ds(index * share, share)
        return pltpu.make_async_copy(terms.at[index], out_ref.at[:, place], out_sems.at[index])

    def keep_copy():
        return pltpu.make_async_copy(atts.at[1], kept_refs[0], out_sems.at[2 * count])

    fetch_att(1).start()
    for index, pair in enumerate(pairs):
        keep = owns(place_ref, pair, chips) == 1
        fetch_carried(2 * index).start()
        for piece in range(pieces):
            pl.when(keep)(fetch_mine(index, piece, True).start)
            pl.when(jnp.logical_not(keep))(fetch_mine(index, piece, False).start)
        if choices == 1:
            fetch_other(index).start()
        else:
            pl.when(keep)(fetch_other(index, 0).start)
            pl.when(jnp.logical_not(keep))(fetch_other(index, 1).start)
        if index == 0:
            fetch_att(0).start()
        fetch_carried(2 * index + 1).start()
    fetch_att(0).wait()
    for index in range(count):
        for piece in range(pieces):
            fetch_mine(index, piece, True).wait()
        for half in range(2):
            columns = slice(half * block, (half + 1) * block)
            corrected = dot_on(mine[index, :, columns], atts[0], 0, 0)
            if half == 0:
                fetch_other(index).wait()
                if index == 0:
                    fetch_att(1).wait()
                    if keep_att:
                        keep_copy().start()
            corrected = corrected + dot_on(other[index, :, columns], atts[1], 0, 0)
            slot = 2 * index + half
            fetch_carried(slot).wait()
            corrected = corrected + carried[slot]
            peak_ref[slot : slot + 1, :] = jnp.max(jnp.abs(corrected), axis=0, keepdims=True)
            rounded = corrected.astype(BF16).reshape(dp_count, share, width)
            if known:
                for group in range(groups):
                    row = (slot * groups + group) * share
                    lanes = slice(group * LANES, (group + 1) * LANES)
                    terms[:, row : row + share, :] = rounded[:, :, lanes]
            else:
                terms[slot] = rounded
            send(slot).start()
    slots = 2 * count
    if known:
        peaks = jnp.concatenate([peak_ref[...]] + [ref[...] for ref in known_refs], 0)
        peaks = jnp.concatenate(
            [peaks[:, group * LANES : (group + 1) * LANES] for group in range(groups)], 0
        ).astype(BF16)
        for dest in range(dp_count):
            terms[dest, slots * groups * share :, :] = peaks
        send(slots).start()
        slots += 1
    for slot in range(slots):
        send(slot).wait()
    if keep_att:
        keep_copy().wait()


def weight_block(place, near, far, recv, att, carried, known, pairs, chips, dp_count, keep_att):
    rows, width = att[0].shape
    block = carried.shape[1]
    share = block // dp_count
    count = len(pairs)
    pieces = len(far[0])
    if known:
        groups = width // LANES
        out_rows = 2 * count * groups * share + 8 * groups
        out_shape = pltpu.HBM((dp_count, out_rows, LANES), BF16)
        terms = pltpu.VMEM((dp_count, out_rows, LANES), BF16)
    else:
        out_shape = pltpu.HBM((dp_count, 2 * count * share, width), BF16)
        terms = pltpu.VMEM((2 * count, dp_count, share, width), BF16)
    vmem = pl.BlockSpec(memory_space=pltpu.VMEM)
    anywhere = pl.BlockSpec(memory_space=pl.ANY)
    hbm = pl.BlockSpec(memory_space=pltpu.HBM)
    return pl.pallas_call(
        functools.partial(
            weight_kernel,
            pairs=pairs,
            pieces=pieces,
            choices=len(recv) // count,
            chips=chips,
            dp_count=dp_count,
            known=len(known),
            keep_att=keep_att,
        ),
        in_specs=[pl.BlockSpec(memory_space=pltpu.SMEM)]
        + [anywhere] * (count * (1 + pieces) + len(recv) + 2)
        + [hbm]
        + [vmem] * len(known),
        out_specs=[hbm, vmem] + [hbm] * keep_att,
        out_shape=[out_shape, jax.ShapeDtypeStruct((2 * count, width), F32)]
        + [pltpu.HBM((rows, width), BF16)] * keep_att,
        scratch_shapes=[
            pltpu.VMEM((2, rows, width), BF16),
            pltpu.VMEM((count, rows, 2 * block), BF16),
            pltpu.VMEM((count, rows, 2 * block), BF16),
            pltpu.VMEM((2 * count, block, width), F32),
            terms,
            pltpu.SemaphoreType.DMA((5, 2 * max(count, 1))),
            pltpu.SemaphoreType.DMA((2 * count + 1,)),
        ],
        compiler_params=pltpu.CompilerParams(vmem_limit_bytes=20 * MIB),
        cost_estimate=cost(0.1),
        name="weight_block",
    )(place, *near, *recv, *[p for f in far for p in f], *att, carried, *known)


def add_kernel(a_ref, b_ref, c_ref, d_ref, first_ref, second_ref):
    first_ref[...] = (a_ref[...].astype(F32) + b_ref[...].astype(F32)).astype(BF16)
    second_ref[...] = (c_ref[...].astype(F32) + d_ref[...].astype(F32)).astype(BF16)


def add_pairs(a, b, c, d):
    rows, width = a.shape
    spec = pl.BlockSpec((rows // 4, width), lambda i: (i, 0))
    return pl.pallas_call(
        add_kernel,
        grid=(4,),
        in_specs=[spec] * 4,
        out_specs=[spec] * 2,
        out_shape=[jax.ShapeDtypeStruct((rows, width), BF16)] * 2,
        compiler_params=pltpu.CompilerParams(vmem_limit_bytes=8 * MIB),
        cost_estimate=cost(0.1),
        name="add_pairs",
    )(a, b, c, d)


def finish_kernel(place_ref, last_ref, sides_ref, middle_ref, levels_ref, scale_ref, *, chips):
    share, width = levels_ref.shape[1:]
    groups = width // LANES
    rows = 2 * groups * share
    total = jnp.sum(last_ref[:, :rows, :].astype(F32), axis=0)
    peaks = jnp.max(last_ref[:, rows:, :].astype(F32), axis=0)
    scale = jnp.concatenate([peaks[group * 8 : group * 8 + 8] for group in range(groups)], 1)
    scale = (scale + 1e-6) / 7.0
    for index, pair in enumerate((0, 1, 3, 2)):
        for half in range(2):
            block = 2 * spot(place_ref, pair, chips) + half
            row = scale[2 * index + half : 2 * index + half + 1]
            scale_ref[pl.ds(block, 1), :] = row
            if pair == 0:
                pieces = [
                    total[(half * groups + group) * share : (half * groups + group + 1) * share]
                    for group in range(groups)
                ]
                terms = jnp.concatenate(pieces, 1)
            else:
                terms_ref = middle_ref if pair == 2 else sides_ref
                start = ((pair == 3) * 2 + half) * share
                terms = terms_ref[pl.ds(start, share), :]
            levels_ref[block] = terms / row


def finish(place, last, sides, middle, share, chips):
    width = middle.shape[1]
    vmem = pl.BlockSpec(memory_space=pltpu.VMEM)
    return pl.pallas_call(
        functools.partial(finish_kernel, chips=chips),
        in_specs=[pl.BlockSpec(memory_space=pltpu.SMEM)] + [vmem] * 3,
        out_specs=[vmem] * 2,
        out_shape=[
            jax.ShapeDtypeStruct((8, share, width), F32),
            jax.ShapeDtypeStruct((8, width), F32),
        ],
        compiler_params=pltpu.CompilerParams(vmem_limit_bytes=12 * MIB),
        cost_estimate=cost(0.1),
        name="finish",
    )(place, last, sides, middle)


def body(query_in, key_in, value_in, attn_grad, out_grad, carried_error, lengths):
    dp_count = lax.axis_size("dp")
    z_count = lax.axis_size("tensor")
    seq = lax.axis_index("seq")
    z = lax.axis_index("tensor")
    up = [(i, (i + 1) % z_count) for i in range(z_count)]
    down = [(i, (i - 1) % z_count) for i in range(z_count)]
    swap = [(0, 1), (1, 0)]

    def peer(array):
        return lax.ppermute(array, "seq", swap)

    own = out_grad[0]
    place = jnp.concatenate([jnp.stack([seq, z]).astype(jnp.int32), lengths[0]])
    heads = own.shape[1] // HEAD_DIM

    def send_up(array):
        return lax.ppermute(array, "tensor", up)

    def send_down(array):
        return lax.ppermute(array, "tensor", down)

    def stay(array):
        return pltpu.with_memory_space_constraint(array, pltpu.HBM)

    from_down, from_up = {1: send_up(own)}, {1: send_down(own)}
    tokens = (
        stay(query_in[0]),
        stay(key_in[0]),
        peer(key_in[0]),
        stay(value_in[0]),
        peer(value_in[0]),
        stay(attn_grad[0]),
    )
    carried = stay(carried_error[0])
    *held, token = attention(place, *tokens, 0, heads // 2, [], [])
    (from_down[1],) = gate([from_down[1]], [token])
    from_down[2] = send_up(from_down[1])
    (from_up[1],) = gate([from_up[1]], [token])
    from_up[2] = send_down(from_up[1])
    att, dq, dk_own, dk_peer, dv_own, dv_peer, token = attention(
        place, *tokens, heads // 2, heads // 2, held, [from_down[1], from_up[1]]
    )
    from_down[2], att = gate([from_down[2], att], [token])
    from_down[3] = send_up(from_down[2])
    (from_up[2],) = gate([from_up[2]], [token])
    from_up[3] = send_down(from_up[2])
    share = carried.shape[1] // dp_count

    def swapped(pair, near, far, after=()):
        return peer(pick_other(place, near, far, pair, z_count, after))

    def weigh(pairs, near, far, recv, atts, known=(), keep_att=False):
        return weight_block(
            place, near, far, recv, atts, carried, known, pairs, z_count, dp_count, keep_att
        )

    def exchange(array):
        return lax.all_to_all(array, "dp", 0, 0, tiled=True)

    recv2 = [peer(from_down[2]), peer(from_up[2])]
    terms, peaks2, att_peer = weigh(
        (2,), [from_down[2]], [[from_up[2]]], recv2, (att, peer(att)), keep_att=True
    )
    atts = (att, stay(att_peer))
    (middle,) = gate([exchange(terms)], [], 1.0)
    from_down[3], from_up[3] = gate([from_down[3], from_up[3]], [peaks2])
    send1, send3, top, bottom = fork(
        place, from_down[3], from_up[3], from_down[1], from_up[1], z_count
    )
    recv13 = [peer(send1), peer(send3)]
    farthest = [send_up(top), send_down(bottom)]
    terms, peaks13 = weigh(
        (1, 3),
        [from_down[1], from_down[3]],
        [[from_up[3]], [from_up[1]]],
        recv13,
        atts,
    )
    farthest = gate(farthest, [peaks13, middle])
    (terms,) = gate([terms], farthest, space=pltpu.HBM)
    (sides,) = gate([exchange(terms)], [])
    recv0 = swapped(0, own, farthest)
    terms, _ = weigh((0,), [own], [farthest], [recv0], atts, (peaks13, peaks2))
    last = exchange(terms)
    d_keys, d_values = add_pairs(dk_own, peer(dk_peer), dv_own, peer(dv_peer))
    level_sums, block_scale = finish(
        place,
        last,
        jnp.sum(sides.astype(F32), axis=0),
        jnp.sum(middle.astype(F32), axis=0),
        share,
        z_count,
    )
    return dq[None], d_keys[None], d_values[None], level_sums, block_scale


def solution(mesh):
    tokens = P("dp", "seq", "tensor")
    in_specs = (tokens,) * 5 + (P("dp", "seq", None, "tensor"), P("dp", None))
    out_specs = (tokens,) * 3 + (P("seq", "dp", "tensor"), P("seq", "tensor"))
    return jax.shard_map(body, mesh=mesh, in_specs=in_specs, out_specs=out_specs, check_vma=False)
```
